32 devices in a mesh: grp: 1, date: 4 (over y, x), shard: 8 (over z, core).
Axes of the slice: x: 2, y: 2, z: 4, core: 2. Of those that a mesh axis runs over, the one named last changes fastest.
Arguments:
- echo_spectra: bfloat16 [4, 2, 128, 8192], P(('grp', 'date'), None, 'shard'), may hold values from -6 to 6
- range_reference: float32 [2, 8192], replicated, may hold values from -5 to 5
- azimuth_reference: bfloat16 [2, 128, 8192], P(None, None, 'shard'), may hold values from -5 to 5
- block_owner: int32 [4, 64], P(('grp', 'date')), may hold values from 0 to 7, as said below
- block_slot: int32 [4, 64], P(('grp', 'date')), may hold values from 0 to 15, as said below
- kernel_index: int32 [4, 64], P(('grp', 'date')), may hold values from 0 to 7
Outputs:
- filtered: bfloat16 [4, 128, 2, 2, 128, 128], P(('grp', 'date'), 'shard')
The draws below stay inside these ranges and needn't reach their ends.
Inputs may be any that keep to these rules, and one draw needn't show every extreme that they name: `block_owner`: every date carries the same owners (the stack is coregistered onto one map grid). Within a date, the 8 blocks of one range-column group name any one owner at most 2 times, and some group names some owner exactly 2 times; every owner is named by at most 16 blocks, and some owner by exactly 16. `block_slot`: every date carries the same slots. Within a date, blocks that name the same owner have distinct slots.
All inputs are finite; a program needn't handle non-finite values.
Results may differ from the reference program's by a relative error of at most 0.017.
Values may be sent and summed in bfloat16 or wider, within the bound.
No kernel may reach another device: no remote copies, remote signals or barrier semaphores. Data moves between devices by JAX's collectives and lax.ppermute only.
A program may use at most 128 MiB of HBM per device.

```python
import math
import jax
import jax.numpy as jnp
from jax import lax

RNG = 8192
RSPLIT = 64
BLK = 128
NSUB = 8
DATES = 4
PULSES = 128
BLK_DEV = 8
BLOCKS = 64
MOST = 2
CAP = 16
TILES = 128
N_SHARD = 8


def slot_shuffle(perm_key):
    return jax.random.permutation(perm_key, CAP).astype(jnp.int32)


def local_shuffle(perm_key):
    return jax.random.permutation(perm_key, BLK_DEV).astype(jnp.int32)


def plan_grid(grid_key):
    keys = jax.random.split(grid_key, 4)
    extra = CAP - BLK_DEV
    swing = jax.random.randint(keys[0], (N_SHARD // 2,), 0, extra + 1).astype(jnp.int32)
    swing = swing.at[0].set(extra)
    loads = jnp.stack([BLK_DEV + swing, BLK_DEV - swing], axis=1).reshape(N_SHARD)
    order = jax.random.permutation(keys[1], N_SHARD).astype(jnp.int32)
    ends = jnp.cumsum(loads).astype(jnp.int32)
    starts = ends - loads
    place = jnp.arange(BLOCKS, dtype=jnp.int32)
    segment = jnp.sum((place[:, None] >= ends[None, :]).astype(jnp.int32), axis=1)
    owner = order[segment]
    rank = place - starts[segment]
    sender = place // MOST % N_SHARD
    local = place // (MOST * N_SHARD) * MOST + place % MOST
    slot_perms = jax.vmap(slot_shuffle)(jax.random.split(keys[2], N_SHARD))
    slot = slot_perms[owner, rank]
    local_perms = jax.vmap(local_shuffle)(jax.random.split(keys[3], N_SHARD))
    target = sender * BLK_DEV + local_perms[sender, local]
    owners = jnp.zeros((BLOCKS,), jnp.int32).at[target].set(owner)
    slots = jnp.zeros((BLOCKS,), jnp.int32).at[target].set(slot)
    return (owners, slots)


def block_plan(key):
    base = jax.random.fold_in(key, 11)
    owners, slots = plan_grid(base)
    return (jnp.broadcast_to(owners[None, :], (DATES, BLOCKS)), jnp.broadcast_to(slots[None, :], (DATES, BLOCKS)))


def draw_block_owner(key, part):
    return block_plan(key)[0]


def draw_block_slot(key, part):
    return block_plan(key)[1]


def with_ends(array, rng, least, high):
    index_at = [jax.random.randint(jax.random.fold_in(rng, axis), (), 0, length) for axis, length in enumerate(array.shape)]
    widest = array.shape.index(max(array.shape))
    neighbour = index_at[:widest] + [(index_at[widest] + 1) % array.shape[widest]] + index_at[widest + 1:]
    return array.at[tuple(index_at)].set(least).at[tuple(neighbour)].set(high)


def shard_levels(key, dims, pieces, smallest, top_value):
    level = 1.0
    for axis_at, blocks in pieces:
        draws = jax.random.uniform(jax.random.fold_in(jax.random.fold_in(key, 6), axis_at), (blocks,), jnp.float32, smallest / len(pieces), top_value / len(pieces))
        level = level * jnp.repeat(jnp.exp(draws), dims[axis_at] // blocks).reshape((-1,) + (1,) * (len(dims) - 1 - axis_at))
    return level


def gaussian(key, dims, deviation, limit, pieces=(), held_as=jnp.bfloat16):
    result = deviation * jax.random.normal(key, dims, jnp.float32)
    if pieces:
        result = result * shard_levels(key, dims, pieces, -0.22, 0.18)
    return jnp.clip(result, -limit, limit).astype(held_as)


def setup_inputs(seed: int = 0, part: int = 0) -> dict:
    key_of = jax.random.split(jax.random.key(seed), 7)
    part_keys = jax.random.split(jax.random.fold_in(key_of[6], part), 7)
    echo_spectra = gaussian(part_keys[0], (DATES, 2, PULSES, RNG), 1.0, 6.0, ((0, 4), (2, 8)))
    range_reference = gaussian(key_of[1], (2, RNG), 0.7, 5.0, (), jnp.float32)
    azimuth_reference = gaussian(key_of[2], (2, PULSES, RNG), 0.7, 5.0, ((2, 8),))
    block_owner = draw_block_owner(jax.random.fold_in(jax.random.fold_in(key_of[6], part), 71), part)
    block_slot = draw_block_slot(jax.random.fold_in(jax.random.fold_in(key_of[6], part), 71), part)
    kernel_index = with_ends(jax.random.randint(part_keys[5], (DATES, BLOCKS), 0, NSUB), jax.random.fold_in(part_keys[5], 1), 0, NSUB - 1).astype(jnp.int32)
    return {"echo_spectra": echo_spectra, "range_reference": range_reference, "azimuth_reference": azimuth_reference, "block_owner": block_owner, "block_slot": block_slot, "kernel_index": kernel_index}


def dft_block(size, sign):
    index = jnp.arange(size, dtype=jnp.int32)
    phase = index[:, None] * index[None, :] % size
    angle = 2.0 * math.pi / size * phase.astype(jnp.float32)
    scale = 1.0 / math.sqrt(size)
    cosine = jnp.cos(angle) * scale
    sine = sign * jnp.sin(angle) * scale
    table = jnp.stack([jnp.stack([cosine, -sine]), jnp.stack([sine, cosine])])
    return jnp.transpose(table, (0, 2, 1, 3)).astype(jnp.bfloat16)

def twiddle(first_len, second_len, total):
    left = jnp.arange(first_len, dtype=jnp.int32)
    right = jnp.arange(second_len, dtype=jnp.int32)
    phase = left[:, None] * right[None, :] % total
    angle = 2.0 * math.pi / total * phase.astype(jnp.float32)
    return (jnp.cos(angle), jnp.sin(angle))

def kernel_table():
    offset = (jnp.arange(NSUB, dtype=jnp.float32) + 0.5) / NSUB
    cells = jnp.arange(BLK, dtype=jnp.float32)
    dist = cells[None, None, :] - cells[None, :, None] - offset[:, None, None]
    window = jnp.where(jnp.abs(dist) < 4.0, 0.5 + 0.5 * jnp.cos(math.pi * dist / 4.0), 0.0)
    return (jnp.sinc(dist) * window).astype(jnp.bfloat16)

def fdot(form, left, right):
    return jnp.einsum(form, left.astype(jnp.float32), right.astype(jnp.float32))

def range_compress(spectra, reference):
    real_in = spectra[0].astype(jnp.float32)
    imag_in = spectra[1].astype(jnp.float32)
    matched = jnp.stack([real_in * reference[0] + imag_in * reference[1], imag_in * reference[0] - real_in * reference[1]]).astype(jnp.bfloat16)
    count = spectra.shape[1]
    outer_len = RSPLIT
    inner_len = RNG // RSPLIT
    shaped = matched.reshape(2, count, outer_len, inner_len)
    section = fdot('cnek,epkb->cpnb', dft_block(outer_len, 1), shaped)
    twc, tws = twiddle(outer_len, inner_len, RNG)
    first = jnp.stack([section[0] * twc - section[1] * tws, section[0] * tws + section[1] * twc]).astype(jnp.bfloat16)
    second = fdot('cmek,epnk->cpmn', dft_block(inner_len, 1), first)
    return second.reshape(2, count, RNG).astype(jnp.bfloat16)

def azimuth_focus(columns, reference):
    count = columns.shape[1]
    doppler = fdot('cuep,epk->cuk', dft_block(count, -1), columns)
    ref_re = reference[0].astype(jnp.float32)
    ref_im = reference[1].astype(jnp.float32)
    shaped = jnp.stack([doppler[0] * ref_re - doppler[1] * ref_im, doppler[0] * ref_im + doppler[1] * ref_re]).astype(jnp.bfloat16)
    return fdot('cuep,epk->cuk', dft_block(count, 1), shaped).astype(jnp.bfloat16)

def cross(first, second):
    fre = first[:, 0].astype(jnp.float32)
    fim = first[:, 1].astype(jnp.float32)
    sre = second[:, 0].astype(jnp.float32)
    sim = second[:, 1].astype(jnp.float32)
    return jnp.stack([fre * sre + fim * sim, fim * sre - fre * sim], axis=1)

def goldstein(patches):
    forward = dft_block(BLK, -1)
    backward = dft_block(BLK, 1)
    rows = fdot('cuei,npeij->npcuj', forward, patches).astype(jnp.bfloat16)
    spectrum = fdot('npeuj,cvej->npcuv', rows, forward)
    power = spectrum[:, :, 0] ** 2 + spectrum[:, :, 1] ** 2
    smooth = jnp.zeros_like(power)
    for down in (-1, 0, 1):
        for across in (-1, 0, 1):
            smooth = smooth + jnp.roll(power, (down, across), axis=(-2, -1))
    smooth = smooth / 9.0
    level = lax.optimization_barrier(jnp.mean(smooth, axis=(-2, -1), keepdims=True))
    weight = jnp.sqrt(jnp.sqrt(smooth / (level + 1e-06)))
    weighted = (spectrum * weight[:, :, None]).astype(jnp.bfloat16)
    back = fdot('cuei,npeij->npcuj', backward, weighted).astype(jnp.bfloat16)
    return fdot('npeuj,cvej->npcuv', back, backward).astype(jnp.bfloat16)

def date_tiles(spectra, range_reference, azimuth_reference, owners, slots, kinds):
    compressed = range_compress(spectra, range_reference)
    image = azimuth_focus(compressed, azimuth_reference)
    row_blocks = PULSES // BLK
    col_blocks = RNG // (N_SHARD * BLK)
    blocks = image.reshape(2, row_blocks, BLK, N_SHARD, col_blocks, BLK)
    blocks = jnp.transpose(blocks, (3, 1, 4, 0, 2, 5)).reshape(BLOCKS, 2, BLK, BLK)
    kernels = kernel_table()[kinds]
    resampled = fdot('nij,ncjk->ncik', kernels, blocks).astype(jnp.bfloat16)
    tiles = jnp.zeros((TILES, 2, BLK, BLK), jnp.bfloat16)
    return tiles.at[owners * CAP + slots].set(resampled)

def reference(echo_spectra, range_reference, azimuth_reference, block_owner, block_slot, kernel_index):
    mapped = [date_tiles(echo_spectra[d], range_reference, azimuth_reference, block_owner[d], block_slot[d], kernel_index[d]) for d in range(DATES)]
    results = []
    for d in range(DATES):
        pairs = jnp.stack([cross(mapped[d], mapped[(d + 1) % DATES]), cross(mapped[d], mapped[(d + 2) % DATES])], axis=1).astype(jnp.bfloat16)
        grouped = pairs.reshape(N_SHARD, CAP, 2, 2, BLK, BLK)
        done = lax.map(goldstein, grouped)
        results.append(done.reshape(TILES, 2, 2, BLK, BLK))
    return jnp.stack(results)
```

```python
import math

import jax
import jax.numpy as jnp
import numpy as np
from jax import lax
from jax.experimental import pallas as pl
from jax.experimental.pallas import tpu as pltpu
from jax.sharding import PartitionSpec as P

BLK = 128
NSUB = 8
BF = jnp.bfloat16
F32 = jnp.float32
VMEM_BYTES = 32 * 1024 * 1024


def dft(rows, cols, size, sign, scale):
    phase = np.outer(np.arange(rows), np.arange(cols)) % size
    angle = 2.0 * np.pi / size * phase
    cosine = np.cos(angle) * scale
    sine = sign * np.sin(angle) * scale
    return np.block([[cosine, -sine], [sine, cosine]])


def kernel_table():
    offset = (np.arange(NSUB) + 0.5) / NSUB
    cells = np.arange(BLK)
    dist = cells[None, None, :] - cells[None, :, None] - offset[:, None, None]
    window = np.where(np.abs(dist) < 4.0, 0.5 + 0.5 * np.cos(np.pi * dist / 4.0), 0.0)
    return np.sinc(dist) * window


def resample_table(pulses):
    inverse = dft(pulses, pulses, pulses, 1, 1.0 / math.sqrt(pulses))
    rows = pulses // BLK
    table = np.zeros((NSUB, rows, 2 * BLK, 2 * pulses))
    kernels = kernel_table()
    for kind in range(NSUB):
        for row in range(rows):
            for part in range(2):
                start = part * pulses + row * BLK
                table[kind, row, part * BLK : (part + 1) * BLK] = (
                    kernels[kind] @ inverse[start : start + BLK]
                )
    return table.reshape(NSUB * rows, 2 * BLK, 2 * pulses)


def const(table):
    return jnp.asarray(table.astype(np.float32)).astype(BF)


def mm(left, right):
    return jnp.dot(left, right, preferred_element_type=F32)


def whole(count):
    return [pl.BlockSpec(memory_space=pltpu.VMEM)] * count


def params():
    return pltpu.CompilerParams(vmem_limit_bytes=VMEM_BYTES)


def is_pow2(count):
    return count & (count - 1) == 0


def target_of(index, step, count):
    if is_pow2(count):
        return index ^ step
    return (index + step) % count


def source_of(index, step, count):
    if is_pow2(count):
        return index ^ step
    return (index + count - step) % count


def hop(value, axis, step):
    count = lax.axis_size(axis)
    return lax.ppermute(value, axis, [(i, target_of(i, step, count)) for i in range(count)])


def shift(value, axis, steps):
    count = lax.axis_size(axis)
    return lax.ppermute(value, axis, [(i, (i + steps) % count) for i in range(count)])


def range_compress(echo, reference, table, me, chunks):
    _, pulses, samples = echo.shape
    shards, capacity = table.shape
    outer = samples // BLK
    each = capacity // chunks
    first = const(dft(outer, outer, outer, 1, 1.0 / math.sqrt(outer)))
    second = const(dft(outer, BLK, outer, 1, 1.0 / math.sqrt(BLK)))
    phase = np.outer(np.arange(BLK), np.arange(BLK)) % samples
    angle = 2.0 * np.pi / samples * phase
    turn = jnp.asarray(np.stack([np.cos(angle), np.sin(angle)]).astype(np.float32))
    spread = BLK // outer

    def kernel(table_ref, me_ref, echo_ref, ref_ref, first_ref, second_ref, turn_ref, *rest):
        outs = rest[: chunks * shards]
        x_re, x_im, y_re, y_im = rest[chunks * shards :]
        for j in range(outer):
            lanes = slice(j * BLK, (j + 1) * BLK)
            a = echo_ref[0, :, lanes].astype(F32)
            b = echo_ref[1, :, lanes].astype(F32)
            c = ref_ref[0:1, lanes]
            d = ref_ref[1:2, lanes]
            x_re[pl.ds(j, pulses, stride=outer), :] = a * c + b * d
            x_im[pl.ds(j, pulses, stride=outer), :] = b * c - a * d
        turn_c = turn_ref[0]
        turn_s = turn_ref[1]
        for q in range(pulses // 2):
            pair = []
            for p in (2 * q, 2 * q + 1):
                rows = slice(p * outer, (p + 1) * outer)
                pair.append(jnp.concatenate([x_re[rows, :], x_im[rows, :]], axis=0))
            section = mm(first_ref[...], jnp.concatenate(pair, axis=1).astype(BF))
            turned = []
            for p in range(2):
                lanes = slice(p * BLK, (p + 1) * BLK)
                re = jnp.concatenate([section[:outer, lanes]] * spread, axis=0)
                im = jnp.concatenate([section[outer:, lanes]] * spread, axis=0)
                turned.append(
                    jnp.concatenate(
                        [re * turn_c - im * turn_s, re * turn_s + im * turn_c], axis=1
                    )
                )
            turned = jnp.concatenate(turned, axis=0).astype(BF)
            done = lax.dot_general(
                second_ref[...], turned, (((1,), (1,)), ((), ())), preferred_element_type=F32
            )
            for p in range(2):
                lanes = slice(p * BLK, (p + 1) * BLK)
                rows = slice((2 * q + p) * outer, (2 * q + p + 1) * outer)
                y_re[rows, :] = done[:outer, lanes]
                y_im[rows, :] = done[outer:, lanes]
        for chunk in range(chunks):
            for k in range(shards):
                owner = target_of(me_ref[0], k, shards)
                out = outs[chunk * shards + k]
                for s in range(each):
                    column = table_ref[owner, chunk * each + s]
                    rows = pl.ds(column, pulses, stride=outer)
                    out[s, 0] = y_re[rows, :].astype(BF)
                    out[s, 1] = y_im[rows, :].astype(BF)

    piece = jax.ShapeDtypeStruct((each, 2, pulses, BLK), BF)
    smem = pl.BlockSpec(memory_space=pltpu.SMEM)
    outs = pl.pallas_call(
        kernel,
        out_shape=[piece] * (chunks * shards),
        in_specs=[smem, smem] + whole(5),
        out_specs=whole(chunks * shards),
        scratch_shapes=[pltpu.VMEM((pulses * outer, BLK), F32)] * 4,
        compiler_params=params(),
        name="range_compress",
    )(table, me, echo, reference, first, second, turn)
    return [outs[chunk * shards : (chunk + 1) * shards] for chunk in range(chunks)]


def filter_columns(reference, table, place, chunks, dates):
    _, doppler, columns = reference.shape
    shards, most = table.shape
    rows = doppler // dates
    each = most // chunks

    def kernel(table_ref, place_ref, ref_ref, *outs):
        start = pl.multiple_of(place_ref[1] * rows, rows)
        for chunk in range(chunks):
            for owner in range(shards):
                for e in range(each):
                    column = table_ref[owner, chunk * each + e]
                    lanes = pl.ds(pl.multiple_of(column * BLK, BLK), BLK)
                    for part in range(2):
                        outs[chunk][owner, e, part] = ref_ref[part, pl.ds(start, rows), lanes]

    smem = pl.BlockSpec(memory_space=pltpu.SMEM)
    piece = jax.ShapeDtypeStruct((shards, each, 2, rows, BLK), BF)
    return pl.pallas_call(
        kernel,
        out_shape=[piece] * chunks,
        in_specs=[smem, smem] + whole(1),
        out_specs=whole(chunks),
        compiler_params=params(),
        name="filter_columns",
    )(table, place, reference)


def focus(pieces, filters, place, entry, kernel_row, valid, subs):
    each, _, share, _ = pieces[0].shape
    shards = len(pieces)
    dates = len(filters)
    pulses = share * shards
    rows = filters[0].shape[-2]
    forward = const(dft(pulses, pulses, pulses, -1, 1.0 / math.sqrt(pulses)))
    back = const(resample_table(pulses))
    per = each // subs

    def kernel(place_ref, entry_ref, row_ref, valid_ref, forward_ref, back_ref, *rest):
        piece_refs = rest[:shards]
        filter_refs = rest[shards : shards + dates]
        outs = rest[shards + dates : shards + dates + subs]
        col, fil = rest[shards + dates + subs :]
        for k in range(shards):
            source = source_of(place_ref[0], k, shards)
            at = pl.multiple_of(source * share, share)
            for s in range(each):
                for part in range(2):
                    col[s, part, pl.ds(at, share), :] = piece_refs[k][s, part]
        for e in range(dates):
            at = pl.multiple_of(source_of(place_ref[1], e, dates) * rows, rows)
            for s in range(each):
                for part in range(2):
                    fil[s, part, pl.ds(at, rows), :] = filter_refs[e][entry_ref[s], part]
        for s in range(0, each, 2):
            both = [col[t].reshape(2 * pulses, BLK) for t in (s, s + 1)]
            doppler = mm(forward_ref[...], jnp.concatenate(both, axis=1))
            for t in (0, 1):
                lanes = slice(t * BLK, (t + 1) * BLK)
                re = doppler[:pulses, lanes]
                im = doppler[pulses:, lanes]
                a = fil[s + t, 0].astype(F32)
                b = fil[s + t, 1].astype(F32)
                shaped = jnp.concatenate([re * a - im * b, re * b + im * a], axis=0).astype(BF)
                image = mm(back_ref[row_ref[s + t]], shaped)
                image = jnp.where(valid_ref[s + t] > 0, image, 0.0).astype(BF)
                out = outs[(s + t) // per]
                out[(s + t) % per, 0] = image[:BLK]
                out[(s + t) % per, 1] = image[BLK:]

    smem = pl.BlockSpec(memory_space=pltpu.SMEM)
    return pl.pallas_call(
        kernel,
        out_shape=[jax.ShapeDtypeStruct((per, 2, BLK, BLK), BF)] * subs,
        in_specs=[smem] * 4 + whole(2 + shards + dates),
        out_specs=whole(subs),
        scratch_shapes=[
            pltpu.VMEM((each, 2, pulses, BLK), BF),
            pltpu.VMEM((each, 2, pulses, BLK), BF),
        ],
        compiler_params=params(),
        name="focus",
    )(place, entry, kernel_row, valid, forward, back, *pieces, *filters)


def goldstein(tile, follows, second, slots, result, capacity):
    count = tile.shape[0]
    scale = 1.0 / math.sqrt(BLK)
    ahead = dft(BLK, BLK, BLK, -1, scale)
    behind = dft(BLK, BLK, BLK, 1, scale)
    tables = [const(ahead), const(ahead.T), const(behind), const(behind.T)]
    have = 0 if result is None else 1

    def sides(left):
        low, high = slice(0, BLK), slice(BLK, 2 * BLK)
        return jnp.concatenate(
            [
                jnp.concatenate([left[low, low], left[high, low]], axis=1),
                jnp.concatenate([left[low, high], left[high, high]], axis=1),
            ],
            axis=0,
        )

    def around(power):
        power = power + (pltpu.roll(power, 1, 0) + pltpu.roll(power, BLK - 1, 0))
        return power + (pltpu.roll(power, 1, 1) + pltpu.roll(power, BLK - 1, 1))

    def kernel(slot_ref, *rest):
        tile_ref, second_ref = rest[:2]
        follow_refs = rest[2 : 2 + len(follows)]
        al_ref, ar_ref, bl_ref, br_ref = rest[2 + len(follows) : 6 + len(follows)]
        out_ref, buffer, sems = rest[6 + len(follows) + have :]
        for s in range(count):
            t_re = tile_ref[s, 0].astype(F32)
            t_im = tile_ref[s, 1].astype(F32)
            f = follow_refs[0][s]
            for other in follow_refs[1:]:
                f = f + other[s]
            pairs = []
            for o in (f, second_ref[s]):
                o_re = o[0].astype(F32)
                o_im = o[1].astype(F32)
                pairs.append((t_re * o_re + t_im * o_im, t_im * o_re - t_re * o_im))
            x = jnp.concatenate(
                [
                    jnp.concatenate([pairs[0][0], pairs[1][0]], axis=1),
                    jnp.concatenate([pairs[0][1], pairs[1][1]], axis=1),
                ],
                axis=0,
            ).astype(BF)
            rows = sides(mm(al_ref[...], x).astype(BF))
            spectrum = mm(rows, ar_ref[...])
            s_re = spectrum[:, :BLK]
            s_im = spectrum[:, BLK:]
            power = s_re * s_re + s_im * s_im
            weights = []
            for p in range(2):
                one = power[p * BLK : (p + 1) * BLK]
                level = jnp.sum(jnp.sum(one, axis=0, keepdims=True), axis=1, keepdims=True)
                inverse = 1.0 / (9.0 * (level * (1.0 / (BLK * BLK)) + 1e-06))
                weights.append(lax.rsqrt(lax.rsqrt(around(one) * inverse)))
            weight = jnp.concatenate(weights, axis=0)
            weighted = jnp.concatenate([s_re * weight, s_im * weight], axis=1).astype(BF)
            back = sides(mm(bl_ref[...], sides(weighted)).astype(BF))
            filtered = mm(back, br_ref[...]).astype(BF)
            for p in range(2):
                for part in range(2):
                    buffer[s, p, part] = filtered[
                        p * BLK : (p + 1) * BLK, part * BLK : (part + 1) * BLK
                    ]
            pltpu.make_async_copy(buffer.at[s], out_ref.at[slot_ref[s]], sems.at[s]).start()
        for s in range(count):
            pltpu.make_async_copy(buffer.at[s], out_ref.at[slot_ref[s]], sems.at[s]).wait()

    anywhere = pl.BlockSpec(memory_space=pl.ANY)
    smem = pl.BlockSpec(memory_space=pltpu.SMEM)
    operands = [slots, tile, second, *follows, *tables] + ([result] if have else [])
    return pl.pallas_call(
        kernel,
        out_shape=jax.ShapeDtypeStruct((capacity, 2, 2, BLK, BLK), BF),
        in_specs=[smem] + whole(6 + len(follows)) + [anywhere] * have,
        out_specs=anywhere,
        scratch_shapes=[
            pltpu.VMEM((count, 2, 2, BLK, BLK), BF),
            pltpu.SemaphoreType.DMA((count,)),
        ],
        input_output_aliases={len(operands) - 1: 0} if have else {},
        compiler_params=params(),
        name="goldstein",
    )(*operands)


def body(echo_spectra, range_reference, azimuth_reference, block_owner, block_slot, kernel_index):
    shards = lax.axis_size("shard")
    dates = lax.axis_size("date")
    me = lax.axis_index("shard")
    date = lax.axis_index("date")
    place = jnp.stack([me, date]).astype(jnp.int32)
    owners, slots, kinds = block_owner[0], block_slot[0], kernel_index[0]
    total = owners.shape[0]
    group = total // shards
    capacity = 2 * group
    most = max(2, capacity // shards)
    pulses = echo_spectra.shape[2] * shards
    group_columns = azimuth_reference.shape[2] // BLK
    row_blocks = pulses // BLK

    numbers = jnp.arange(total, dtype=jnp.int32)
    sender = numbers // group
    column = numbers % group % group_columns
    row = numbers % group // group_columns
    earlier = (
        (sender[:, None] == sender[None, :])
        & (owners[:, None] == owners[None, :])
        & (numbers[None, :] < numbers[:, None])
    )
    rank = jnp.sum(earlier.astype(jnp.int32), axis=1)
    by_rank = shards * most == capacity
    chunks = most if by_rank else 1
    each = capacity // chunks
    where = rank * shards + sender if by_rank else slots
    at = owners * capacity + where
    cells = jnp.arange(shards * capacity, dtype=jnp.int32)
    found = at[None, :] == cells[:, None]
    columns = jnp.sum(jnp.where(found, (sender * group_columns + column)[None, :], 0), axis=1)
    columns = columns.reshape(shards, capacity)
    mine = (owners[None, :] == me) & (where[None, :] == jnp.arange(capacity)[:, None])

    def of_mine(values):
        return jnp.sum(jnp.where(mine, values[None, :], 0), axis=1)

    valid = of_mine(jnp.ones_like(numbers))
    kernel_row = of_mine(kinds * row_blocks + row)
    entry = of_mine(sender * (most // chunks) + rank % (most // chunks))
    named = of_mine(slots)
    used = jnp.sum(
        ((named[None, :] == jnp.arange(capacity)[:, None]) & (valid > 0)[None, :]).astype(jnp.int32),
        axis=1,
    )
    lower = jnp.arange(capacity)[None, :] < jnp.arange(capacity)[:, None]
    empty_rank = jnp.sum(jnp.where(lower, 1 - valid[None, :], 0), axis=1)
    free_rank = jnp.sum(jnp.where(lower, 1 - used[None, :], 0), axis=1)
    free = (free_rank[None, :] == empty_rank[:, None]) & (used == 0)[None, :]
    spare = jnp.sum(jnp.where(free, jnp.arange(capacity)[None, :], 0), axis=1)
    slot_of = jnp.where(valid > 0, named, spare)

    hits = (
        (sender == me)[None, :]
        & ((owners * most + rank)[None, :] == jnp.arange(shards * most)[:, None])
    )
    filter_table = jnp.sum(jnp.where(hits, column[None, :], 0), axis=1).reshape(shards, most)

    shares = filter_columns(azimuth_reference, filter_table, place, chunks, dates)
    filters = []
    for share in shares:
        got = lax.all_to_all(share, "shard", split_axis=0, concat_axis=0, tiled=True)
        got = got.reshape((shards * (most // chunks),) + got.shape[2:])
        filters.append([got] + [hop(got, "date", e) for e in range(1, dates)])

    outbox = range_compress(echo_spectra[0], range_reference, columns, place, chunks)
    subs = 2
    per = each // subs
    result = None
    for chunk in range(chunks):
        pieces = [outbox[chunk][0]] + [
            hop(outbox[chunk][k], "shard", k) for k in range(1, shards)
        ]
        span = slice(chunk * each, (chunk + 1) * each)
        tiles = focus(
            pieces, filters[chunk], place, entry[span], kernel_row[span], valid[span], subs
        )
        for sub, tile in enumerate(tiles):
            if dates == 4:
                second = hop(tile, "date", 2)
                follows = [
                    lax.ppermute(tile, "date", [(1, 0), (3, 2)]),
                    lax.ppermute(second, "date", [(0, 1), (2, 3)]),
                ]
            else:
                second = shift(tile, "date", -2)
                follows = [shift(tile, "date", -1)]
            start = chunk * each + sub * per
            result = goldstein(
                tile, follows, second, slot_of[start : start + per], result, capacity
            )
    return result[None]


def solution(mesh):
    in_specs = (
        P(("grp", "date"), None, "shard", None),
        P(),
        P(None, None, "shard"),
        P(("grp", "date"), None),
        P(("grp", "date"), None),
        P(("grp", "date"), None),
    )
    out_specs = P(("grp", "date"), "shard", None, None, None, None)
    return jax.shard_map(body, mesh=mesh, in_specs=in_specs, out_specs=out_specs, check_vma=False)
```

```python
import math

import jax
import jax.numpy as jnp
import numpy as np
from jax import lax
from jax.experimental import pallas as pl
from jax.experimental.pallas import tpu as pltpu
from jax.sharding import PartitionSpec as P

BLK = 128
NSUB = 8
BF = jnp.bfloat16
F32 = jnp.float32
MIB = 1024 * 1024
K1_MIB = 56


def dft(rows, cols, size, sign, scale):
    phase = np.outer(np.arange(rows), np.arange(cols)) % size
    angle = 2.0 * np.pi / size * phase
    cosine = np.cos(angle) * scale
    sine = sign * np.sin(angle) * scale
    return np.block([[cosine, -sine], [sine, cosine]])


def kernel_table():
    offset = (np.arange(NSUB) + 0.5) / NSUB
    cells = np.arange(BLK)
    dist = cells[None, None, :] - cells[None, :, None] - offset[:, None, None]
    window = np.where(np.abs(dist) < 4.0, 0.5 + 0.5 * np.cos(np.pi * dist / 4.0), 0.0)
    return np.sinc(dist) * window


def resample_table(pulses):
    inverse = dft(pulses, pulses, pulses, 1, 1.0 / math.sqrt(pulses))
    rows = pulses // BLK
    table = np.zeros((NSUB, rows, 2 * BLK, 2 * pulses))
    kernels = kernel_table()
    for kind in range(NSUB):
        for row in range(rows):
            for part in range(2):
                start = part * pulses + row * BLK
                table[kind, row, part * BLK : (part + 1) * BLK] = (
                    kernels[kind] @ inverse[start : start + BLK]
                )
    return table.reshape(NSUB * rows, 2 * BLK, 2 * pulses)


def const(table):
    return jnp.asarray(table.astype(np.float32)).astype(BF)


def mm(left, right):
    return jnp.dot(left, right, preferred_element_type=F32)


def whole(count):
    return [pl.BlockSpec(memory_space=pltpu.VMEM)] * count


def loaded(arrays):
    def spec(shape):
        return pl.BlockSpec(shape, lambda *_: (0,) * len(shape))

    return [spec(a.shape) for a in arrays]


def params(mib):
    return pltpu.CompilerParams(vmem_limit_bytes=mib * MIB)


def cost(macs, arrays):
    size = sum(math.prod(a.shape) * a.dtype.itemsize for a in arrays)
    return pl.CostEstimate(flops=2 * macs, bytes_accessed=size, transcendentals=0)


def is_pow2(count):
    return count & (count - 1) == 0


def target_of(index, step, count):
    if is_pow2(count):
        return index ^ step
    return (index + step) % count


def source_of(index, step, count):
    if is_pow2(count):
        return index ^ step
    return (index + count - step) % count


def step_from(index, source, count):
    if is_pow2(count):
        return index ^ source
    return (index + count - source) % count


def hop(value, axis, step, within=None):
    count = lax.axis_size(axis)
    if within is None and axis == "shard" and count % 2 == 0:
        pairs = [(i, target_of(i // 2, step // 2, count // 2) * 2 + i % 2) for i in range(count)]
    else:
        size = within or count
        pairs = [(i, i // size * size + target_of(i % size, step, size)) for i in range(count)]
    return lax.ppermute(value, axis, pairs)


def shift(value, axis, steps):
    count = lax.axis_size(axis)
    return lax.ppermute(value, axis, [(i, (i + steps) % count) for i in range(count)])


def position(rank, sender, slot, shards, most, capacity):
    if shards * most == capacity:
        return rank * shards + sender
    return slot


def range_compress(echo, reference, owners, slots, place, plan):
    _, pulses, samples = echo.shape
    shards, capacity, most, group, group_columns = plan
    total = owners.shape[0]
    outer = samples // BLK
    first = const(dft(outer, outer, outer, 1, 1.0 / math.sqrt(outer)))
    second = const(dft(outer, BLK, outer, 1, 1.0 / math.sqrt(BLK)))
    phase = np.outer(np.arange(BLK), np.arange(BLK)) % samples
    angle = 2.0 * np.pi / samples * phase
    turn = jnp.asarray(np.stack([np.cos(angle), np.sin(angle)]).astype(np.float32))
    spread = BLK // outer
    operands = [echo, reference, first, second, turn]
    smem = pl.BlockSpec(memory_space=pltpu.SMEM)

    def arrange(owner_ref, slot_ref, place_ref, block_ref, out_slot_ref, count_ref, free_ref):
        for o in range(shards):
            for w in range(capacity):
                block_ref[o, w] = 0
            for g in range(shards):
                count_ref[g, o] = 0
        for b in range(total):
            g = b // group
            owner = owner_ref[b]
            rank = count_ref[g, owner]
            count_ref[g, owner] = rank + 1
            where = position(rank, g, slot_ref[b], shards, most, capacity)
            block_ref[owner, where] = (b + 1) * most + rank
        me = place_ref[0]
        for w in range(capacity):
            free_ref[w] = 0
        for w in range(capacity):
            code = block_ref[me, w] // most
            slot = slot_ref[jnp.maximum(code - 1, 0)]
            out_slot_ref[w] = jnp.where(code > 0, slot, -1)
            free_ref[jnp.where(code > 0, slot, capacity)] = 1
        spare = 0
        for w in range(capacity):
            taken = free_ref[w]
            free_ref[capacity + 1 + spare] = w
            spare = spare + 1 - taken
        spare = 0
        for w in range(capacity):
            slot = out_slot_ref[w]
            out_slot_ref[w] = jnp.where(slot < 0, free_ref[capacity + 1 + spare], slot)
            spare = spare + jnp.where(slot < 0, 1, 0)

    def kernel(owner_ref, slot_ref, place_ref, *refs):
        count = len(operands)
        out_ref, block_ref, out_slot_ref = refs[count : count + 3]
        local = refs[count + 3 : 2 * count + 3]
        x_re, x_im, y_re, y_im, sems, count_ref, free_ref = refs[2 * count + 3 :]
        copies = [
            pltpu.make_async_copy(refs[i], local[i], sems.at[i]) for i in range(count)
        ]
        for copy in copies:
            copy.start()
        arrange(owner_ref, slot_ref, place_ref, block_ref, out_slot_ref, count_ref, free_ref)
        for copy in copies:
            copy.wait()
        echo_ref, ref_ref, first_ref, second_ref, turn_ref = local
        for j in range(outer):
            lanes = slice(j * BLK, (j + 1) * BLK)
            a = echo_ref[0, :, lanes].astype(F32)
            b = echo_ref[1, :, lanes].astype(F32)
            c = ref_ref[0:1, lanes]
            d = ref_ref[1:2, lanes]
            x_re[pl.ds(j, pulses, stride=outer), :] = a * c + b * d
            x_im[pl.ds(j, pulses, stride=outer), :] = b * c - a * d
        turn_c = turn_ref[0]
        turn_s = turn_ref[1]
        for q in range(pulses // 2):
            pair = []
            for p in (2 * q, 2 * q + 1):
                rows = slice(p * outer, (p + 1) * outer)
                pair.append(jnp.concatenate([x_re[rows, :], x_im[rows, :]], axis=0))
            section = mm(first_ref[...], jnp.concatenate(pair, axis=1).astype(BF))
            turned = []
            for p in range(2):
                lanes = slice(p * BLK, (p + 1) * BLK)
                re = jnp.concatenate([section[:outer, lanes]] * spread, axis=0)
                im = jnp.concatenate([section[outer:, lanes]] * spread, axis=0)
                turned.append(
                    jnp.concatenate(
                        [re * turn_c - im * turn_s, re * turn_s + im * turn_c], axis=1
                    )
                )
            turned = jnp.concatenate(turned, axis=0).astype(BF)
            done = lax.dot_general(
                second_ref[...], turned, (((1,), (1,)), ((), ())), preferred_element_type=F32
            )
            for p in range(2):
                lanes = slice(p * BLK, (p + 1) * BLK)
                rows = slice((2 * q + p) * outer, (2 * q + p + 1) * outer)
                y_re[rows, :] = done[:outer, lanes]
                y_im[rows, :] = done[outer:, lanes]
        for j in range(outer):
            rows = pl.ds(j, pulses, stride=outer)
            out_ref[0, j] = y_re[rows, :].astype(BF)
            out_ref[1, j] = y_im[rows, :].astype(BF)

    return pl.pallas_call(
        kernel,
        out_shape=[
            jax.ShapeDtypeStruct((2, outer, pulses, BLK), BF),
            jax.ShapeDtypeStruct((shards, capacity), jnp.int32),
            jax.ShapeDtypeStruct((capacity,), jnp.int32),
        ],
        in_specs=[smem] * 3 + [pl.BlockSpec(memory_space=pl.ANY)] * len(operands),
        out_specs=[pl.BlockSpec(memory_space=pltpu.VMEM)] + [smem] * 2,
        scratch_shapes=[pltpu.VMEM(a.shape, a.dtype) for a in operands]
        + [pltpu.VMEM((pulses * outer, BLK), F32)] * 4
        + [
            pltpu.SemaphoreType.DMA((len(operands),)),
            pltpu.SMEM((shards, shards), jnp.int32),
            pltpu.SMEM((2 * capacity + 2,), jnp.int32),
        ],
        compiler_params=params(K1_MIB),
        cost_estimate=cost(
            pulses * 4 * BLK * outer * (outer + BLK), [echo, echo, echo, reference, turn]
        ),
        name="range_compress",
    )(owners, slots, place, *operands)


def spread_columns(parts, table, place, chunks, plan):
    _, _, pulses, _ = parts[0].shape
    cores = len(parts)
    shards, capacity, most, group, group_columns = plan
    chips = shards // cores
    each = capacity // chunks

    def kernel(table_ref, place_ref, *rest):
        part_refs = rest[:cores]
        outs = rest[cores:]
        chip = place_ref[0] // cores
        core = place_ref[0] % cores
        for chunk in range(chunks):
            for k in range(chips):
                owner = target_of(chip, k, chips) * cores + core
                out = outs[chunk * chips + k]
                for s in range(each):
                    block = jnp.maximum(table_ref[owner, chunk * each + s] // most - 1, 0)
                    column = block // group * group_columns + block % group % group_columns
                    for c in range(cores):
                        at = source_of(core, c, cores) * pulses
                        rows = pl.ds(pl.multiple_of(at, pulses), pulses)
                        out[s, 0, rows, :] = part_refs[c][0, column]
                        out[s, 1, rows, :] = part_refs[c][1, column]

    piece = jax.ShapeDtypeStruct((each, 2, cores * pulses, BLK), BF)
    smem = pl.BlockSpec(memory_space=pltpu.SMEM)
    outs = pl.pallas_call(
        kernel,
        out_shape=[piece] * (chunks * chips),
        in_specs=[smem, smem] + whole(cores),
        out_specs=whole(chunks * chips),
        compiler_params=params(16),
        cost_estimate=cost(0, [*parts] * 2),
        name="spread_columns",
    )(table, place, *parts)
    return [outs[chunk * chips : (chunk + 1) * chips] for chunk in range(chunks)]


def filter_columns(parts, owners, place, plan):
    _, rows, columns = parts[0].shape
    cores = len(parts)
    shards, _, most, group, group_columns = plan
    chips = shards // cores

    def kernel(owner_ref, place_ref, *rest):
        part_refs = rest[:cores]
        outs = rest[cores : cores + chips]
        column_ref, count_ref = rest[cores + chips :]
        chip = place_ref[0] // cores
        core = place_ref[0] % cores
        for c in range(cores):
            for o in range(shards):
                count_ref[c, o] = 0
                for r in range(most):
                    column_ref[c, o * most + r] = 0
            for b in range(group):
                owner = owner_ref[(chip * cores + c) * group + b]
                rank = count_ref[c, owner]
                count_ref[c, owner] = rank + 1
                column_ref[c, owner * most + rank] = b % group_columns
        for k in range(chips):
            owner = target_of(chip, k, chips) * cores + core
            for c in range(cores):
                at = source_of(core, c, cores)
                for e in range(most):
                    column = column_ref[at, owner * most + e]
                    lanes = pl.ds(pl.multiple_of(column * BLK, BLK), BLK)
                    for part in range(2):
                        outs[k][at * most + e, part] = part_refs[c][part, :, lanes]

    piece = jax.ShapeDtypeStruct((cores * most, 2, rows, BLK), BF)
    smem = pl.BlockSpec(memory_space=pltpu.SMEM)
    return pl.pallas_call(
        kernel,
        out_shape=[piece] * chips,
        in_specs=[smem, smem] + whole(cores),
        out_specs=whole(chips),
        scratch_shapes=[
            pltpu.SMEM((cores, shards * most), jnp.int32),
            pltpu.SMEM((cores, shards), jnp.int32),
        ],
        compiler_params=params(16),
        cost_estimate=cost(0, [*parts] * 2),
        name="filter_columns",
    )(owners, place, *parts)


def focus(pieces, filters, place, table, kinds, start, cores, subs, plan):
    each, _, share, _ = pieces[0].shape
    chips = len(pieces)
    dates = len(filters)
    pulses = share * chips
    rows = filters[0].shape[-2]
    forward = const(dft(pulses, pulses, pulses, -1, 1.0 / math.sqrt(pulses)))
    back = const(resample_table(pulses))
    per = each // subs

    _, _, most, group, group_columns = plan

    def kernel(place_ref, table_ref, kind_ref, forward_ref, back_ref, *rest):
        piece_refs = rest[:chips]
        filter_refs = rest[chips : chips + dates]
        outs = rest[chips + dates : chips + dates + subs]
        col, fil = rest[chips + dates + subs :]
        chip = place_ref[0] // cores
        entries, table_rows, valid = [], [], []
        for s in range(each):
            code = table_ref[place_ref[0], start + s]
            block = code // most - 1
            valid.append(block >= 0)
            block = jnp.maximum(block, 0)
            sender = block // group
            step = step_from(chip, sender // cores, chips)
            entries.append((step * cores + sender % cores) * most + code % most)
            table_rows.append(kind_ref[block] * (pulses // BLK) + block % group // group_columns)
        for k in range(chips):
            source = source_of(chip, k, chips)
            at = pl.multiple_of(source * share, share)
            for s in range(each):
                for part in range(2):
                    col[s, part, pl.ds(at, share), :] = piece_refs[k][s, part]
        for e in range(dates):
            at = pl.multiple_of(source_of(place_ref[1], e, dates) * rows, rows)
            for s in range(each):
                for part in range(2):
                    fil[s, part, pl.ds(at, rows), :] = filter_refs[e][entries[s], part]
        for s in range(0, each, 2):
            both = [col[t].reshape(2 * pulses, BLK) for t in (s, s + 1)]
            doppler = mm(forward_ref[...], jnp.concatenate(both, axis=1))
            for t in (0, 1):
                lanes = slice(t * BLK, (t + 1) * BLK)
                re = doppler[:pulses, lanes]
                im = doppler[pulses:, lanes]
                a = fil[s + t, 0].astype(F32)
                b = fil[s + t, 1].astype(F32)
                shaped = jnp.concatenate([re * a - im * b, re * b + im * a], axis=0).astype(BF)
                image = mm(back_ref[table_rows[s + t]], shaped)
                image = jnp.where(valid[s + t], image, 0.0).astype(BF)
                out = outs[(s + t) // per]
                out[(s + t) % per, 0] = image[:BLK]
                out[(s + t) % per, 1] = image[BLK:]

    smem = pl.BlockSpec(memory_space=pltpu.SMEM)
    return pl.pallas_call(
        kernel,
        out_shape=[jax.ShapeDtypeStruct((per, 2, BLK, BLK), BF)] * subs,
        in_specs=[smem] * 3 + whole(2 + chips + dates),
        out_specs=whole(subs),
        scratch_shapes=[
            pltpu.VMEM((each, 2, pulses, BLK), BF),
            pltpu.VMEM((each, 2, pulses, BLK), BF),
        ],
        compiler_params=params(16),
        cost_estimate=cost(
            each * 4 * pulses * (pulses + BLK) * BLK, [*pieces, *filters, forward, back]
        ),
        name="focus",
    )(place, table, kinds, forward, back, *pieces, *filters)


def goldstein(tiles, follows, seconds, slots, start, result):
    sizes = [tile.shape[0] for tile in tiles]
    count = sum(sizes)
    homes = [(i, s) for i, size in enumerate(sizes) for s in range(size)]
    capacity = slots.shape[0]
    scale = 1.0 / math.sqrt(BLK)
    ahead = dft(BLK, BLK, BLK, -1, scale)
    behind = dft(BLK, BLK, BLK, 1, scale)
    tables = [const(ahead), const(ahead.T), const(behind), const(behind.T)]
    have = 0 if result is None else 1
    batch = 4

    def aside(left):
        pairs = left.shape[1] // BLK
        return jnp.concatenate(
            [
                jnp.concatenate(
                    [left[:BLK, p * BLK : (p + 1) * BLK], left[BLK:, p * BLK : (p + 1) * BLK]],
                    axis=1,
                )
                for p in range(pairs)
            ],
            axis=0,
        )

    def around(power):
        power = power + (pltpu.roll(power, 1, 0) + pltpu.roll(power, BLK - 1, 0))
        return power + (pltpu.roll(power, 1, 1) + pltpu.roll(power, BLK - 1, 1))

    def kernel(slot_ref, *rest):
        many = len(tiles)
        tile_refs, follow_refs, second_refs = (rest[i * many : (i + 1) * many] for i in range(3))
        al_ref, ar_ref, bl_ref, br_ref = rest[3 * many : 3 * many + 4]
        out_ref, buffer, sems = rest[3 * many + 4 + have :]
        for base in range(0, count, batch):
            batched = range(base, min(base + batch, count))
            pairs = []
            for s in batched:
                i, at = homes[s]
                t_re = tile_refs[i][at, 0].astype(F32)
                t_im = tile_refs[i][at, 1].astype(F32)
                for o in (follow_refs[i][at], second_refs[i][at]):
                    o_re = o[0].astype(F32)
                    o_im = o[1].astype(F32)
                    re = (t_re * o_re + t_im * o_im).astype(BF)
                    im = (t_im * o_re - t_re * o_im).astype(BF)
                    pairs.append(jnp.concatenate([re, im], axis=0))
            rows = aside(mm(al_ref[...], jnp.concatenate(pairs, axis=1)).astype(BF))
            spectrum = mm(rows, ar_ref[...])
            weighted = []
            for p in range(len(pairs)):
                s_re = spectrum[p * BLK : (p + 1) * BLK, :BLK]
                s_im = spectrum[p * BLK : (p + 1) * BLK, BLK:]
                power = s_re * s_re + s_im * s_im
                level = jnp.sum(jnp.sum(power, axis=0, keepdims=True), axis=1, keepdims=True)
                inverse = 1.0 / (9.0 * (level * (1.0 / (BLK * BLK)) + 1e-06))
                weight = lax.rsqrt(lax.rsqrt(around(power) * inverse))
                weighted.append(
                    jnp.concatenate([(s_re * weight).astype(BF), (s_im * weight).astype(BF)], axis=0)
                )
            back = aside(mm(bl_ref[...], jnp.concatenate(weighted, axis=1)).astype(BF))
            filtered = mm(back, br_ref[...]).astype(BF)
            for p in range(len(pairs)):
                for part in range(2):
                    buffer[base + p // 2, p % 2, part] = filtered[
                        p * BLK : (p + 1) * BLK, part * BLK : (part + 1) * BLK
                    ]
            for s in batched:
                pltpu.make_async_copy(buffer.at[s], out_ref.at[slot_ref[start + s]], sems.at[s]).start()
        for s in range(count):
            pltpu.make_async_copy(buffer.at[s], out_ref.at[slot_ref[start + s]], sems.at[s]).wait()

    anywhere = pl.BlockSpec(memory_space=pl.ANY)
    smem = pl.BlockSpec(memory_space=pltpu.SMEM)
    operands = [slots, *tiles, *follows, *seconds, *tables] + ([result] if have else [])
    return pl.pallas_call(
        kernel,
        out_shape=jax.ShapeDtypeStruct((capacity, 2, 2, BLK, BLK), BF),
        in_specs=[smem] + whole(3 * len(tiles) + 4) + [anywhere] * have,
        out_specs=anywhere,
        scratch_shapes=[
            pltpu.VMEM((count, 2, 2, BLK, BLK), BF),
            pltpu.SemaphoreType.DMA((count,)),
        ],
        input_output_aliases={len(operands) - 1: 0} if have else {},
        compiler_params=params(16),
        cost_estimate=cost(count * 2 * 4 * 4 * BLK**3, operands + [*seconds] * 2),
        name="goldstein",
    )(*operands)


def body(echo_spectra, range_reference, azimuth_reference, block_owner, block_slot, kernel_index):
    shards = lax.axis_size("shard")
    dates = lax.axis_size("date")
    me = lax.axis_index("shard")
    date = lax.axis_index("date")
    place = jnp.stack([me, date]).astype(jnp.int32)
    owners, slots, kinds = block_owner[0], block_slot[0], kernel_index[0]
    cores = 2 if shards % 2 == 0 else 1
    chips = shards // cores
    total = owners.shape[0]
    group = total // shards
    capacity = 2 * group
    most = max(2, capacity // shards)
    group_columns = azimuth_reference.shape[2] // BLK
    plan = (shards, capacity, most, group, group_columns)
    chunks = most if shards * most == capacity else 1
    each = capacity // chunks

    rows = azimuth_reference.shape[1] // dates
    share = lax.dynamic_slice_in_dim(azimuth_reference, date * rows, rows, axis=1)
    shares = [share] + [hop(share, "shard", c, cores) for c in range(1, cores)]
    sent = filter_columns(shares, owners, place, plan)
    echo = echo_spectra[0]
    echo, sent = lax.optimization_barrier((echo, sent))
    got = [sent[0]] + [hop(sent[k], "shard", k * cores) for k in range(1, chips)]
    got = jnp.concatenate(got, axis=0)
    filters = [got] + [hop(got, "date", e) for e in range(1, dates)]
    compressed, blocks, slot_of = range_compress(
        echo, range_reference, owners, slots, place, plan
    )
    parts = [compressed] + [hop(compressed, "shard", c, cores) for c in range(1, cores)]
    outbox = spread_columns(parts, blocks, place, chunks, plan)
    splits = (4, 2)
    tiles, follows, seconds = [], [], []
    for chunk in range(chunks):
        pieces = [outbox[chunk][0]] + [
            hop(outbox[chunk][k], "shard", k * cores) for k in range(1, chips)
        ]
        if chunk > 0 and 1 > 0:
            pieces, kept = lax.optimization_barrier((pieces, follows[0][:1]))
            follows[0][:1] = kept
        subs = splits[chunk] if each % (2 * splits[chunk]) == 0 else 1
        mine = focus(pieces, filters, place, blocks, kinds, chunk * each, cores, subs, plan)
        tiles.append(mine)
        follows.append([])
        seconds.append([])
        for tile in mine:
            if dates == 4:
                second = hop(tile, "date", 2)
                follow = hop(jnp.where(date % 2 == 0, second, tile), "date", 1)
            else:
                second = shift(tile, "date", -2)
                follow = shift(tile, "date", -1)
            follows[-1].append(follow)
            seconds[-1].append(second)
    result = None
    start = 0
    for chunk in range(chunks):
        last = chunk == chunks - 1
        parts = [slice(i, i + 1) for i in range(len(tiles[chunk]))] if last else [slice(None)]
        for part in parts:
            mine = tiles[chunk][part]
            result = goldstein(
                mine, follows[chunk][part], seconds[chunk][part], slot_of, start, result
            )
            start += sum(tile.shape[0] for tile in mine)
    return result[None]


def solution(mesh):
    in_specs = (
        P(("grp", "date"), None, "shard", None),
        P(),
        P(None, None, "shard"),
        P(("grp", "date"), None),
        P(("grp", "date"), None),
        P(("grp", "date"), None),
    )
    out_specs = P(("grp", "date"), "shard", None, None, None, None)
    return jax.shard_map(body, mesh=mesh, in_specs=in_specs, out_specs=out_specs, check_vma=False)
```

```python
import math

import jax
import jax.numpy as jnp
import numpy as np
from jax import lax
from jax.experimental import pallas as pl
from jax.experimental.pallas import tpu as pltpu
from jax.sharding import PartitionSpec as P

BLK = 128
NSUB = 8
BF = jnp.bfloat16
F32 = jnp.float32
MIB = 1024 * 1024
K1_MIB = 56


def dft(rows, cols, size, sign, scale):
    phase = np.outer(np.arange(rows), np.arange(cols)) % size
    angle = 2.0 * np.pi / size * phase
    cosine = np.cos(angle) * scale
    sine = sign * np.sin(angle) * scale
    return np.block([[cosine, -sine], [sine, cosine]])


def kernel_table():
    offset = (np.arange(NSUB) + 0.5) / NSUB
    cells = np.arange(BLK)
    dist = cells[None, None, :] - cells[None, :, None] - offset[:, None, None]
    window = np.where(np.abs(dist) < 4.0, 0.5 + 0.5 * np.cos(np.pi * dist / 4.0), 0.0)
    return np.sinc(dist) * window


def resample_table(pulses):
    inverse = dft(pulses, pulses, pulses, 1, 1.0 / math.sqrt(pulses))
    rows = pulses // BLK
    table = np.zeros((NSUB, rows, 2 * BLK, 2 * pulses))
    kernels = kernel_table()
    for kind in range(NSUB):
        for row in range(rows):
            for part in range(2):
                start = part * pulses + row * BLK
                table[kind, row, part * BLK : (part + 1) * BLK] = (
                    kernels[kind] @ inverse[start : start + BLK]
                )
    return table.reshape(NSUB * rows, 2 * BLK, 2 * pulses)


def const(table):
    return jnp.asarray(table.astype(np.float32)).astype(BF)


def mm(left, right):
    return jnp.dot(left, right, preferred_element_type=F32)


def whole(count):
    return [pl.BlockSpec(memory_space=pltpu.VMEM)] * count


def loaded(arrays):
    def spec(shape):
        return pl.BlockSpec(shape, lambda *_: (0,) * len(shape))

    return [spec(a.shape) for a in arrays]


def params(mib):
    return pltpu.CompilerParams(vmem_limit_bytes=mib * MIB)


def cost(macs, arrays):
    size = sum(math.prod(a.shape) * a.dtype.itemsize for a in arrays)
    return pl.CostEstimate(flops=int(2 * macs), bytes_accessed=size, transcendentals=0)


def is_pow2(count):
    return count & (count - 1) == 0


def target_of(index, step, count):
    if is_pow2(count):
        return index ^ step
    return (index + step) % count


def source_of(index, step, count):
    if is_pow2(count):
        return index ^ step
    return (index + count - step) % count


def step_from(index, source, count):
    if is_pow2(count):
        return index ^ source
    return (index + count - source) % count


def hop(value, axis, step, within=None):
    count = lax.axis_size(axis)
    if within is None and axis == "shard" and count % 2 == 0:
        pairs = [(i, target_of(i // 2, step // 2, count // 2) * 2 + i % 2) for i in range(count)]
    else:
        size = within or count
        pairs = [(i, i // size * size + target_of(i % size, step, size)) for i in range(count)]
    return lax.ppermute(value, axis, pairs)


def shift(value, axis, steps):
    count = lax.axis_size(axis)
    return lax.ppermute(value, axis, [(i, (i + steps) % count) for i in range(count)])


def range_compress(echo, reference, owners, slots, plan):
    _, pulses, samples = echo.shape
    shards, capacity, most, group, group_columns = plan
    total = owners.shape[0]
    outer = samples // BLK
    first = const(dft(outer, outer, outer, 1, 1.0 / math.sqrt(outer)))
    second = const(dft(outer, BLK, outer, 1, 1.0 / math.sqrt(BLK)))
    phase = np.outer(np.arange(BLK), np.arange(BLK)) % samples
    angle = 2.0 * np.pi / samples * phase
    turn = jnp.asarray(np.stack([np.cos(angle), np.sin(angle)]).astype(np.float32))
    spread = BLK // outer
    operands = [echo, reference, first, second, turn]
    smem = pl.BlockSpec(memory_space=pltpu.SMEM)

    def arrange(owner_ref, slot_ref, block_ref, place_ref, count_ref):
        for o in range(shards):
            for w in range(capacity):
                block_ref[o, w] = 0
                place_ref[o, w] = 0
            for g in range(shards):
                count_ref[g, o] = 0
        for b in range(total):
            owner = owner_ref[b]
            rank = count_ref[b // group, owner]
            count_ref[b // group, owner] = rank + 1
            slot = slot_ref[b]
            block_ref[owner, slot] = (b + 1) * most + rank
            place_ref[owner, slot] = b // group * group_columns + b % group % group_columns

    def kernel(owner_ref, slot_ref, *refs):
        count = len(operands)
        out_ref, block_ref, place_ref = refs[count : count + 3]
        local = refs[count + 3 : 2 * count + 3]
        x_re, x_im, y_re, y_im, sems, count_ref = refs[2 * count + 3 :]
        copies = [
            pltpu.make_async_copy(refs[i], local[i], sems.at[i]) for i in range(count)
        ]
        for copy in copies:
            copy.start()
        arrange(owner_ref, slot_ref, block_ref, place_ref, count_ref)
        for copy in copies:
            copy.wait()
        echo_ref, ref_ref, first_ref, second_ref, turn_ref = local
        for j in range(outer):
            lanes = slice(j * BLK, (j + 1) * BLK)
            a = echo_ref[0, :, lanes].astype(F32)
            b = echo_ref[1, :, lanes].astype(F32)
            c = ref_ref[0:1, lanes]
            d = ref_ref[1:2, lanes]
            x_re[pl.ds(j, pulses, stride=outer), :] = a * c + b * d
            x_im[pl.ds(j, pulses, stride=outer), :] = b * c - a * d
        turn_c = turn_ref[0]
        turn_s = turn_ref[1]
        for q in range(pulses // 2):
            pair = []
            for p in (2 * q, 2 * q + 1):
                rows = slice(p * outer, (p + 1) * outer)
                pair.append(jnp.concatenate([x_re[rows, :], x_im[rows, :]], axis=0))
            section = mm(first_ref[...], jnp.concatenate(pair, axis=1).astype(BF))
            turned = []
            for p in range(2):
                lanes = slice(p * BLK, (p + 1) * BLK)
                re = jnp.concatenate([section[:outer, lanes]] * spread, axis=0)
                im = jnp.concatenate([section[outer:, lanes]] * spread, axis=0)
                turned.append(
                    jnp.concatenate(
                        [re * turn_c - im * turn_s, re * turn_s + im * turn_c], axis=1
                    )
                )
            turned = jnp.concatenate(turned, axis=0).astype(BF)
            done = lax.dot_general(
                second_ref[...], turned, (((1,), (1,)), ((), ())), preferred_element_type=F32
            )
            for p in range(2):
                lanes = slice(p * BLK, (p + 1) * BLK)
                rows = slice((2 * q + p) * outer, (2 * q + p + 1) * outer)
                y_re[rows, :] = done[:outer, lanes]
                y_im[rows, :] = done[outer:, lanes]
        for j in range(outer):
            rows = pl.ds(j, pulses, stride=outer)
            out_ref[0, j] = y_re[rows, :].astype(BF)
            out_ref[1, j] = y_im[rows, :].astype(BF)

    return pl.pallas_call(
        kernel,
        out_shape=[
            jax.ShapeDtypeStruct((2, outer, pulses, BLK), BF),
            jax.ShapeDtypeStruct((shards, capacity), jnp.int32),
            jax.ShapeDtypeStruct((shards, capacity), jnp.int32),
        ],
        in_specs=[smem] * 2 + [pl.BlockSpec(memory_space=pl.ANY)] * len(operands),
        out_specs=[pl.BlockSpec(memory_space=pltpu.VMEM), smem, smem],
        scratch_shapes=[pltpu.VMEM(a.shape, a.dtype) for a in operands]
        + [pltpu.VMEM((pulses * outer, BLK), F32)] * 4
        + [
            pltpu.SemaphoreType.DMA((len(operands),)),
            pltpu.SMEM((shards, shards), jnp.int32),
        ],
        compiler_params=params(K1_MIB),
        cost_estimate=cost(
            pulses * 4 * BLK * outer * (outer + BLK), [echo, echo, echo, reference, turn]
        ),
        name="range_compress",
    )(owners, slots, *operands)


def spread_columns(parts, table, place, sizes, plan):
    _, _, pulses, _ = parts[0].shape
    cores = len(parts)
    shards, capacity, most, group, group_columns = plan
    chips = shards // cores
    chunks = len(sizes)

    def kernel(table_ref, place_ref, *rest):
        part_refs = rest[:cores]
        outs = rest[cores:]
        chip = place_ref[0] // cores
        core = place_ref[0] % cores
        for chunk in range(chunks):
            for k in range(chips):
                owner = target_of(chip, k, chips) * cores + core
                out = outs[chunk * chips + k]
                for s in range(sizes[chunk]):
                    column = table_ref[owner, sum(sizes[:chunk]) + s]
                    for c in range(cores):
                        at = source_of(core, c, cores) * pulses
                        rows = pl.ds(pl.multiple_of(at, pulses), pulses)
                        out[s, 0, rows, :] = part_refs[c][0, column]
                        out[s, 1, rows, :] = part_refs[c][1, column]

    pieces = [jax.ShapeDtypeStruct((size, 2, cores * pulses, BLK), BF) for size in sizes]
    smem = pl.BlockSpec(memory_space=pltpu.SMEM)
    outs = pl.pallas_call(
        kernel,
        out_shape=[piece for piece in pieces for _ in range(chips)],
        in_specs=[smem, smem] + whole(cores),
        out_specs=whole(chunks * chips),
        compiler_params=params(16),
        cost_estimate=cost(0, [*parts] * 2),
        name="spread_columns",
    )(table, place, *parts)
    return [outs[chunk * chips : (chunk + 1) * chips] for chunk in range(chunks)]


def filter_columns(parts, owners, place, plan):
    _, rows, columns = parts[0].shape
    cores = len(parts)
    shards, _, most, group, group_columns = plan
    chips = shards // cores

    def kernel(owner_ref, place_ref, *rest):
        part_refs = rest[:cores]
        outs = rest[cores : cores + chips]
        column_ref, count_ref = rest[cores + chips :]
        chip = place_ref[0] // cores
        core = place_ref[0] % cores
        for c in range(cores):
            for o in range(shards):
                count_ref[c, o] = 0
                for r in range(most):
                    column_ref[c, o * most + r] = 0
            for b in range(group):
                owner = owner_ref[(chip * cores + c) * group + b]
                rank = count_ref[c, owner]
                count_ref[c, owner] = rank + 1
                column_ref[c, owner * most + rank] = b % group_columns
        for k in range(chips):
            owner = target_of(chip, k, chips) * cores + core
            for c in range(cores):
                at = source_of(core, c, cores)
                for e in range(most):
                    column = column_ref[at, owner * most + e]
                    lanes = pl.ds(pl.multiple_of(column * BLK, BLK), BLK)
                    for part in range(2):
                        outs[k][at * most + e, part] = part_refs[c][part, :, lanes]

    piece = jax.ShapeDtypeStruct((cores * most, 2, rows, BLK), BF)
    smem = pl.BlockSpec(memory_space=pltpu.SMEM)
    return pl.pallas_call(
        kernel,
        out_shape=[piece] * chips,
        in_specs=[smem, smem] + whole(cores),
        out_specs=whole(chips),
        scratch_shapes=[
            pltpu.SMEM((cores, shards * most), jnp.int32),
            pltpu.SMEM((cores, shards), jnp.int32),
        ],
        compiler_params=params(16),
        cost_estimate=cost(0, [*parts] * 2),
        name="filter_columns",
    )(owners, place, *parts)


def focus(pieces, filters, place, table, kinds, start, cores, sizes, plan):
    each, _, share, _ = pieces[0].shape
    chips = len(pieces)
    dates = len(filters)
    pulses = share * chips
    rows = filters[0].shape[-2]
    forward = const(dft(pulses, pulses, pulses, -1, 1.0 / math.sqrt(pulses)))
    back = const(resample_table(pulses))

    _, _, most, group, group_columns = plan

    def kernel(place_ref, table_ref, kind_ref, forward_ref, back_ref, *rest):
        piece_refs = rest[:chips]
        filter_refs = rest[chips : chips + dates]
        outs = rest[chips + dates : chips + dates + len(sizes)]
        col, fil = rest[chips + dates + len(sizes) :]
        homes = [(i, s) for i, size in enumerate(sizes) for s in range(size)]
        chip = place_ref[0] // cores
        entries, table_rows, valid = [], [], []
        for s in range(each):
            code = table_ref[place_ref[0], start + s]
            block = code // most - 1
            valid.append(block >= 0)
            block = jnp.maximum(block, 0)
            sender = block // group
            step = step_from(chip, sender // cores, chips)
            entries.append((step * cores + sender % cores) * most + code % most)
            table_rows.append(kind_ref[block] * (pulses // BLK) + block % group // group_columns)
        for k in range(chips):
            source = source_of(chip, k, chips)
            at = pl.multiple_of(source * share, share)
            for s in range(each):
                for part in range(2):
                    col[s, part, pl.ds(at, share), :] = piece_refs[k][s, part]
        for e in range(dates):
            at = pl.multiple_of(source_of(place_ref[1], e, dates) * rows, rows)
            for s in range(each):
                for part in range(2):
                    fil[s, part, pl.ds(at, rows), :] = filter_refs[e][entries[s], part]
        for s in range(0, each, 2):
            both = [col[t].reshape(2 * pulses, BLK) for t in (s, s + 1)]
            doppler = mm(forward_ref[...], jnp.concatenate(both, axis=1))
            for t in (0, 1):
                lanes = slice(t * BLK, (t + 1) * BLK)
                re = doppler[:pulses, lanes]
                im = doppler[pulses:, lanes]
                a = fil[s + t, 0].astype(F32)
                b = fil[s + t, 1].astype(F32)
                shaped = jnp.concatenate([re * a - im * b, re * b + im * a], axis=0).astype(BF)
                image = mm(back_ref[table_rows[s + t]], shaped)
                image = jnp.where(valid[s + t], image, 0.0).astype(BF)
                i, at = homes[s + t]
                outs[i][at, 0] = image[:BLK]
                outs[i][at, 1] = image[BLK:]

    smem = pl.BlockSpec(memory_space=pltpu.SMEM)
    return pl.pallas_call(
        kernel,
        out_shape=[jax.ShapeDtypeStruct((size, 2, BLK, BLK), BF) for size in sizes],
        in_specs=[smem] * 3 + whole(2 + chips + dates),
        out_specs=whole(len(sizes)),
        scratch_shapes=[
            pltpu.VMEM((each, 2, pulses, BLK), BF),
            pltpu.VMEM((each, 2, pulses, BLK), BF),
        ],
        compiler_params=params(16),
        cost_estimate=cost(
            4 * each * 4 * pulses * (pulses + BLK) * BLK, [*pieces, *filters, forward, back] * 4
        ),
        name="focus",
    )(place, table, kinds, forward, back, *pieces, *filters)


def goldstein(tiles, follows, seconds, start, capacity, result):
    sizes = [tile.shape[0] for tile in tiles]
    count = sum(sizes)
    homes = [(i, s) for i, size in enumerate(sizes) for s in range(size)]
    scale = 1.0 / math.sqrt(BLK)
    ahead = dft(BLK, BLK, BLK, -1, scale)
    behind = dft(BLK, BLK, BLK, 1, scale)
    tables = [const(ahead), const(ahead.T), const(behind), const(behind.T)]
    have = 0 if result is None else 1
    batch = 4

    def aside(left):
        pairs = left.shape[1] // BLK
        return jnp.concatenate(
            [
                jnp.concatenate(
                    [left[:BLK, p * BLK : (p + 1) * BLK], left[BLK:, p * BLK : (p + 1) * BLK]],
                    axis=1,
                )
                for p in range(pairs)
            ],
            axis=0,
        )

    def around(power):
        power = power + (pltpu.roll(power, 1, 0) + pltpu.roll(power, BLK - 1, 0))
        return power + (pltpu.roll(power, 1, 1) + pltpu.roll(power, BLK - 1, 1))

    def kernel(*rest):
        many = len(tiles)
        tile_refs, follow_refs, second_refs = (rest[i * many : (i + 1) * many] for i in range(3))
        al_ref, ar_ref, bl_ref, br_ref = rest[3 * many : 3 * many + 4]
        out_ref, buffer, sems = rest[3 * many + 4 + have :]
        for base in range(0, count, batch):
            batched = range(base, min(base + batch, count))
            pairs = []
            for s in batched:
                i, at = homes[s]
                t_re = tile_refs[i][at, 0].astype(F32)
                t_im = tile_refs[i][at, 1].astype(F32)
                for o in (follow_refs[i][at], second_refs[i][at]):
                    o_re = o[0].astype(F32)
                    o_im = o[1].astype(F32)
                    re = (t_re * o_re + t_im * o_im).astype(BF)
                    im = (t_im * o_re - t_re * o_im).astype(BF)
                    pairs.append(jnp.concatenate([re, im], axis=0))
            rows = aside(mm(al_ref[...], jnp.concatenate(pairs, axis=1)).astype(BF))
            spectrum = mm(rows, ar_ref[...])
            weighted = []
            for p in range(len(pairs)):
                s_re = spectrum[p * BLK : (p + 1) * BLK, :BLK]
                s_im = spectrum[p * BLK : (p + 1) * BLK, BLK:]
                power = s_re * s_re + s_im * s_im
                level = jnp.sum(jnp.sum(power, axis=0, keepdims=True), axis=1, keepdims=True)
                inverse = 1.0 / (9.0 * (level * (1.0 / (BLK * BLK)) + 1e-06))
                weight = lax.rsqrt(lax.rsqrt(around(power) * inverse))
                weighted.append(
                    jnp.concatenate([(s_re * weight).astype(BF), (s_im * weight).astype(BF)], axis=0)
                )
            back = aside(mm(bl_ref[...], jnp.concatenate(weighted, axis=1)).astype(BF))
            filtered = mm(back, br_ref[...]).astype(BF)
            for p in range(len(pairs)):
                for part in range(2):
                    buffer[base + p // 2, p % 2, part] = filtered[
                        p * BLK : (p + 1) * BLK, part * BLK : (part + 1) * BLK
                    ]
            for s in batched:
                pltpu.make_async_copy(buffer.at[s], out_ref.at[start + s], sems.at[s]).start()
        for s in range(count):
            pltpu.make_async_copy(buffer.at[s], out_ref.at[start + s], sems.at[s]).wait()

    anywhere = pl.BlockSpec(memory_space=pl.ANY)
    operands = [*tiles, *follows, *seconds, *tables] + ([result] if have else [])
    return pl.pallas_call(
        kernel,
        out_shape=jax.ShapeDtypeStruct((capacity, 2, 2, BLK, BLK), BF),
        in_specs=whole(3 * len(tiles) + 4) + [anywhere] * have,
        out_specs=anywhere,
        scratch_shapes=[
            pltpu.VMEM((count, 2, 2, BLK, BLK), BF),
            pltpu.SemaphoreType.DMA((count,)),
        ],
        input_output_aliases={len(operands) - 1: 0} if have else {},
        compiler_params=params(16),
        cost_estimate=cost(count * 2 * 4 * 4 * BLK**3, operands + [*seconds] * 2),
        name="goldstein",
    )(*operands)


def body(echo_spectra, range_reference, azimuth_reference, block_owner, block_slot, kernel_index):
    shards = lax.axis_size("shard")
    dates = lax.axis_size("date")
    me = lax.axis_index("shard")
    date = lax.axis_index("date")
    place = jnp.stack([me, date]).astype(jnp.int32)
    owners, slots, kinds = block_owner[0], block_slot[0], kernel_index[0]
    cores = 2 if shards % 2 == 0 else 1
    chips = shards // cores
    total = owners.shape[0]
    group = total // shards
    capacity = 2 * group
    most = max(2, capacity // shards)
    group_columns = azimuth_reference.shape[2] // BLK
    plan = (shards, capacity, most, group, group_columns)
    rows = azimuth_reference.shape[1] // dates
    share = lax.dynamic_slice_in_dim(azimuth_reference, date * rows, rows, axis=1)
    shares = [share] + [hop(share, "shard", c, cores) for c in range(1, cores)]
    sent = filter_columns(shares, owners, place, plan)
    echo = echo_spectra[0]
    echo, sent = lax.optimization_barrier((echo, sent))
    got = [sent[0]] + [hop(sent[k], "shard", k * cores) for k in range(1, chips)]
    got = jnp.concatenate(got, axis=0)
    filters = [got] + [hop(got, "date", e) for e in range(1, dates)]
    compressed, blocks, columns = range_compress(echo, range_reference, owners, slots, plan)
    parts = [compressed] + [hop(compressed, "shard", c, cores) for c in range(1, cores)]
    splits = ((2, 2, 2, 2), (4, 4)) if capacity == 16 else ((capacity,),)
    outbox = spread_columns(parts, columns, place, [sum(sizes) for sizes in splits], plan)
    tiles, follows, seconds = [], [], []
    start = 0
    for chunk, sizes in enumerate(splits):
        pieces = [outbox[chunk][0]] + [
            hop(outbox[chunk][k], "shard", k * cores) for k in range(1, chips)
        ]
        mine = focus(pieces, filters, place, blocks, kinds, start, cores, sizes, plan)
        start += sum(sizes)
        if chunk:
            mine, follows[:1] = lax.optimization_barrier((mine, follows[:1]))
        for tile in mine:
            if dates == 4:
                second = hop(tile, "date", 2)
                follow = hop(jnp.where(date % 2 == 0, second, tile), "date", 1)
            else:
                second = shift(tile, "date", -2)
                follow = shift(tile, "date", -1)
            tiles.append(tile)
            follows.append(follow)
            seconds.append(second)
    result = None
    start = 0
    groups = [4, 1, 1] if len(tiles) == 6 else [len(tiles)]
    for group in groups:
        take = slice(0, group)
        mine = tiles[take], follows[take], seconds[take]
        result = goldstein(*mine, start, capacity, result)
        start += sum(tile.shape[0] for tile in mine[0])
        del tiles[take], follows[take], seconds[take]
    return result[None]


def solution(mesh):
    in_specs = (
        P(("grp", "date"), None, "shard", None),
        P(),
        P(None, None, "shard"),
        P(("grp", "date"), None),
        P(("grp", "date"), None),
        P(("grp", "date"), None),
    )
    out_specs = P(("grp", "date"), "shard", None, None, None, None)
    return jax.shard_map(body, mesh=mesh, in_specs=in_specs, out_specs=out_specs, check_vma=False)
```

```python
import math

import jax
import jax.numpy as jnp
import numpy as np
from jax import lax
from jax.experimental import pallas as pl
from jax.experimental.pallas import tpu as pltpu
from jax.sharding import PartitionSpec as P

BLK = 128
NSUB = 8
BF = jnp.bfloat16
F32 = jnp.float32
MIB = 1024 * 1024


def dft(rows, cols, size, sign, scale):
    phase = np.outer(np.arange(rows), np.arange(cols)) % size
    angle = 2.0 * np.pi / size * phase
    cosine = np.cos(angle) * scale
    sine = sign * np.sin(angle) * scale
    return np.block([[cosine, -sine], [sine, cosine]])


def kernel_table():
    offset = (np.arange(NSUB) + 0.5) / NSUB
    cells = np.arange(BLK)
    dist = cells[None, None, :] - cells[None, :, None] - offset[:, None, None]
    window = np.where(np.abs(dist) < 4.0, 0.5 + 0.5 * np.cos(np.pi * dist / 4.0), 0.0)
    return np.sinc(dist) * window


def resample_table(pulses):
    inverse = dft(pulses, pulses, pulses, 1, 1.0 / math.sqrt(pulses))
    rows = pulses // BLK
    table = np.zeros((NSUB, rows, 2 * BLK, 2 * pulses))
    kernels = kernel_table()
    for kind in range(NSUB):
        for row in range(rows):
            for part in range(2):
                start = part * pulses + row * BLK
                table[kind, row, part * BLK : (part + 1) * BLK] = (
                    kernels[kind] @ inverse[start : start + BLK]
                )
    return table.reshape(NSUB * rows, 2 * BLK, 2 * pulses)


def const(table):
    return jnp.asarray(table.astype(np.float32)).astype(BF)


def mm(left, right):
    return jnp.dot(left, right, preferred_element_type=F32)


def whole(count):
    return [pl.BlockSpec(memory_space=pltpu.VMEM)] * count


def loaded(arrays):
    def spec(shape):
        return pl.BlockSpec(shape, lambda *_: (0,) * len(shape))

    return [spec(a.shape) for a in arrays]


def params(mib):
    return pltpu.CompilerParams(vmem_limit_bytes=mib * MIB)


def cost(macs, arrays):
    size = sum(math.prod(a.shape) * a.dtype.itemsize for a in arrays)
    return pl.CostEstimate(flops=int(2 * macs), bytes_accessed=size, transcendentals=0)


def is_pow2(count):
    return count & (count - 1) == 0


def target_of(index, step, count):
    if is_pow2(count):
        return index ^ step
    return (index + step) % count


def source_of(index, step, count):
    if is_pow2(count):
        return index ^ step
    return (index + count - step) % count


def step_from(index, source, count):
    if is_pow2(count):
        return index ^ source
    return (index + count - source) % count


def hop(value, axis, step, within=None):
    count = lax.axis_size(axis)
    if within is None and axis == "shard" and count % 2 == 0:
        pairs = [(i, target_of(i // 2, step // 2, count // 2) * 2 + i % 2) for i in range(count)]
    else:
        size = within or count
        pairs = [(i, i // size * size + target_of(i % size, step, size)) for i in range(count)]
    return lax.ppermute(value, axis, pairs)


def shift(value, axis, steps):
    count = lax.axis_size(axis)
    return lax.ppermute(value, axis, [(i, (i + steps) % count) for i in range(count)])


def range_compress(real, imag, info, plan):
    pulses, samples = real.shape
    shards, capacity, most, group, group_columns = plan
    total = shards * group
    outer = samples // BLK
    first = dft(outer, outer, outer, 1, 1.0 / math.sqrt(outer))
    second = dft(outer, BLK, outer, 1, 1.0 / math.sqrt(BLK))
    phase = np.outer(np.arange(BLK), np.arange(BLK)) % samples
    angle = 2.0 * np.pi / samples * phase
    first = np.pad(first, ((0, 0), (0, BLK - 2 * outer)))
    rows = [np.cos(angle), np.sin(angle), first, second[:, :BLK], second[:, BLK:]]
    tables = jnp.asarray(np.concatenate(rows).astype(np.float32))
    spread = BLK // outer
    smem = pl.BlockSpec(memory_space=pltpu.SMEM)

    def arrange(info_ref, block_ref, place_ref, count_ref):
        for o in range(shards):
            for w in range(capacity):
                block_ref[o, w] = 0
                place_ref[o, w] = 0
            for g in range(shards):
                count_ref[g, o] = 0
        for b in range(total):
            owner = info_ref[b]
            rank = count_ref[b // group, owner]
            count_ref[b // group, owner] = rank + 1
            slot = info_ref[total + b]
            block_ref[owner, slot] = (b + 1) * most + rank
            place_ref[owner, slot] = b // group * group_columns + b % group % group_columns

    def kernel(info_ref, real_ref, imag_ref, tables_ref, *rest):
        out_ref, block_ref, place_ref, x_re, x_im, y_re, y_im, count_ref = rest
        arrange(info_ref, block_ref, place_ref, count_ref)
        at = 2 * BLK
        first_table = tables_ref[at : at + 2 * outer, : 2 * outer].astype(BF)
        at += 2 * outer
        second_table = jnp.concatenate(
            [tables_ref[at : at + 2 * outer, :], tables_ref[at + 2 * outer : at + 4 * outer, :]],
            axis=1,
        ).astype(BF)
        for j in range(outer):
            lanes = slice(j * BLK, (j + 1) * BLK)
            x_re[pl.ds(j, pulses, stride=outer), :] = real_ref[:, lanes].astype(F32)
            x_im[pl.ds(j, pulses, stride=outer), :] = imag_ref[:, lanes].astype(F32)
        turn_c = tables_ref[:BLK, :]
        turn_s = tables_ref[BLK : 2 * BLK, :]
        for q in range(pulses // 2):
            pair = []
            for p in (2 * q, 2 * q + 1):
                rows = slice(p * outer, (p + 1) * outer)
                pair.append(jnp.concatenate([x_re[rows, :], x_im[rows, :]], axis=0))
            section = mm(first_table, jnp.concatenate(pair, axis=1).astype(BF))
            turned = []
            for p in range(2):
                lanes = slice(p * BLK, (p + 1) * BLK)
                re = jnp.concatenate([section[:outer, lanes]] * spread, axis=0)
                im = jnp.concatenate([section[outer:, lanes]] * spread, axis=0)
                turned.append(
                    jnp.concatenate(
                        [re * turn_c - im * turn_s, re * turn_s + im * turn_c], axis=1
                    )
                )
            turned = jnp.concatenate(turned, axis=0).astype(BF)
            done = lax.dot_general(
                second_table, turned, (((1,), (1,)), ((), ())), preferred_element_type=F32
            )
            for p in range(2):
                lanes = slice(p * BLK, (p + 1) * BLK)
                rows = slice((2 * q + p) * outer, (2 * q + p + 1) * outer)
                y_re[rows, :] = done[:outer, lanes]
                y_im[rows, :] = done[outer:, lanes]
        for j in range(outer):
            rows = pl.ds(j, pulses, stride=outer)
            out_ref[0, j] = y_re[rows, :].astype(BF)
            out_ref[1, j] = y_im[rows, :].astype(BF)

    return pl.pallas_call(
        kernel,
        out_shape=[
            jax.ShapeDtypeStruct((2, outer, pulses, BLK), BF),
            jax.ShapeDtypeStruct((shards, capacity), jnp.int32),
            jax.ShapeDtypeStruct((shards, capacity), jnp.int32),
        ],
        in_specs=[smem] + whole(3),
        out_specs=[pl.BlockSpec(memory_space=pltpu.VMEM), smem, smem],
        scratch_shapes=[pltpu.VMEM((pulses * outer, BLK), F32)] * 4
        + [
            pltpu.SMEM((shards, shards), jnp.int32),
        ],
        compiler_params=params(16),
        cost_estimate=cost(
            pulses * 4 * BLK * outer * (outer + BLK), [real] * 6 + [tables]
        ),
        name="range_compress",
    )(info, real, imag, tables)


def spread_columns(parts, table, info, sizes, plan):
    _, _, pulses, _ = parts[0].shape
    cores = len(parts)
    shards, capacity, most, group, group_columns = plan
    chips = shards // cores
    chunks = len(sizes)

    def kernel(table_ref, info_ref, *rest):
        part_refs = rest[:cores]
        outs = rest[cores:]
        chip = info_ref[3 * shards * group] // cores
        core = info_ref[3 * shards * group] % cores
        for chunk in range(chunks):
            for k in range(chips):
                owner = target_of(chip, k, chips) * cores + core
                out = outs[chunk * chips + k]
                for s in range(sizes[chunk]):
                    column = table_ref[owner, sum(sizes[:chunk]) + s]
                    for c in range(cores):
                        at = source_of(core, c, cores) * pulses
                        rows = pl.ds(pl.multiple_of(at, pulses), pulses)
                        out[s, 0, rows, :] = part_refs[c][0, column]
                        out[s, 1, rows, :] = part_refs[c][1, column]

    pieces = [jax.ShapeDtypeStruct((size, 2, cores * pulses, BLK), BF) for size in sizes]
    smem = pl.BlockSpec(memory_space=pltpu.SMEM)
    outs = pl.pallas_call(
        kernel,
        out_shape=[piece for piece in pieces for _ in range(chips)],
        in_specs=[smem, smem] + whole(cores),
        out_specs=whole(chunks * chips),
        compiler_params=params(16),
        cost_estimate=cost(0, [*parts] * 2),
        name="spread_columns",
    )(table, info, *parts)
    return [outs[chunk * chips : (chunk + 1) * chips] for chunk in range(chunks)]


def filter_columns(parts, info, plan):
    _, rows, columns = parts[0].shape
    cores = len(parts)
    shards, _, most, group, group_columns = plan
    chips = shards // cores

    def kernel(info_ref, *rest):
        part_refs = rest[:cores]
        outs = rest[cores : cores + chips]
        column_ref, count_ref = rest[cores + chips :]
        chip = info_ref[3 * shards * group] // cores
        core = info_ref[3 * shards * group] % cores
        for c in range(cores):
            for o in range(shards):
                count_ref[c, o] = 0
                for r in range(most):
                    column_ref[c, o * most + r] = 0
            for b in range(group):
                owner = info_ref[(chip * cores + c) * group + b]
                rank = count_ref[c, owner]
                count_ref[c, owner] = rank + 1
                column_ref[c, owner * most + rank] = b % group_columns
        for k in range(chips):
            owner = target_of(chip, k, chips) * cores + core
            for c in range(cores):
                at = source_of(core, c, cores)
                for e in range(most):
                    column = column_ref[at, owner * most + e]
                    lanes = pl.ds(pl.multiple_of(column * BLK, BLK), BLK)
                    for part in range(2):
                        outs[k][at * most + e, part] = part_refs[c][part, :, lanes]

    piece = jax.ShapeDtypeStruct((cores * most, 2, rows, BLK), BF)
    smem = pl.BlockSpec(memory_space=pltpu.SMEM)
    return pl.pallas_call(
        kernel,
        out_shape=[piece] * chips,
        in_specs=[smem] + whole(cores),
        out_specs=whole(chips),
        scratch_shapes=[
            pltpu.SMEM((cores, shards * most), jnp.int32),
            pltpu.SMEM((cores, shards), jnp.int32),
        ],
        compiler_params=params(16),
        cost_estimate=cost(0, [*parts] * 2),
        name="filter_columns",
    )(info, *parts)


def focus(pieces, filters, table, info, start, cores, sizes, plan, flip):
    each, _, share, _ = pieces[0].shape
    chips = len(pieces)
    dates = len(filters)
    pulses = share * chips
    rows = filters[0].shape[-2]
    forward = const(dft(pulses, pulses, pulses, -1, 1.0 / math.sqrt(pulses)))
    back = resample_table(pulses)
    last = len(back) - 1
    back = const(back[::-1] if flip else back)

    shards, _, most, group, group_columns = plan

    def kernel(info_ref, table_ref, forward_ref, back_ref, *rest):
        piece_refs = rest[:chips]
        filter_refs = rest[chips : chips + dates]
        outs = rest[chips + dates : chips + dates + len(sizes)]
        col, fil = rest[chips + dates + len(sizes) :]
        homes = [(i, s) for i, size in enumerate(sizes) for s in range(size)]
        chip = info_ref[3 * shards * group] // cores
        entries, table_rows, valid = [], [], []
        for s in range(each):
            code = table_ref[info_ref[3 * shards * group], start + s]
            block = code // most - 1
            valid.append(block >= 0)
            block = jnp.maximum(block, 0)
            sender = block // group
            step = step_from(chip, sender // cores, chips)
            entries.append((step * cores + sender % cores) * most + code % most)
            row = info_ref[2 * shards * group + block] * (pulses // BLK)
            row = row + block % group // group_columns
            table_rows.append(last - row if flip else row)
        for k in range(chips):
            source = source_of(chip, k, chips)
            at = pl.multiple_of(source * share, share)
            for s in range(each):
                for part in range(2):
                    col[s, part, pl.ds(at, share), :] = piece_refs[k][s, part]
        for e in range(dates):
            at = pl.multiple_of(source_of(info_ref[3 * shards * group + 1], e, dates) * rows, rows)
            for s in range(each):
                for part in range(2):
                    fil[s, part, pl.ds(at, rows), :] = filter_refs[e][entries[s], part]
        for s in range(0, each, 2):
            both = [col[t].reshape(2 * pulses, BLK) for t in (s, s + 1)]
            doppler = mm(forward_ref[...], jnp.concatenate(both, axis=1))
            for t in (0, 1):
                lanes = slice(t * BLK, (t + 1) * BLK)
                re = doppler[:pulses, lanes]
                im = doppler[pulses:, lanes]
                a = fil[s + t, 0].astype(F32)
                b = fil[s + t, 1].astype(F32)
                shaped = jnp.concatenate([re * a - im * b, re * b + im * a], axis=0).astype(BF)
                image = mm(back_ref[table_rows[s + t]], shaped)
                image = jnp.where(valid[s + t], image, 0.0).astype(BF)
                i, at = homes[s + t]
                outs[i][at, 0] = image[:BLK]
                outs[i][at, 1] = image[BLK:]

    smem = pl.BlockSpec(memory_space=pltpu.SMEM)
    return pl.pallas_call(
        kernel,
        out_shape=[jax.ShapeDtypeStruct((size, 2, BLK, BLK), BF) for size in sizes],
        in_specs=[smem] * 2 + whole(2 + chips + dates),
        out_specs=whole(len(sizes)),
        scratch_shapes=[
            pltpu.VMEM((each, 2, pulses, BLK), BF),
            pltpu.VMEM((each, 2, pulses, BLK), BF),
        ],
        compiler_params=params(16),
        cost_estimate=cost(
            4 * each * 4 * pulses * (pulses + BLK) * BLK, [*pieces, *filters, forward, back] * 4
        ),
        name="focus",
    )(info, table, forward, back, *pieces, *filters)


def goldstein(tiles, follows, seconds, start, capacity, result):
    sizes = [tile.shape[0] for tile in tiles]
    count = sum(sizes)
    homes = [(i, s) for i, size in enumerate(sizes) for s in range(size)]
    scale = 1.0 / math.sqrt(BLK)
    ahead = dft(BLK, BLK, BLK, -1, scale)
    behind = dft(BLK, BLK, BLK, 1, scale)
    tables = [const(ahead), const(ahead.T), const(behind), const(behind.T)]
    have = 0 if result is None else 1
    batch = 4

    def aside(left):
        pairs = left.shape[1] // BLK
        return jnp.concatenate(
            [
                jnp.concatenate(
                    [left[:BLK, p * BLK : (p + 1) * BLK], left[BLK:, p * BLK : (p + 1) * BLK]],
                    axis=1,
                )
                for p in range(pairs)
            ],
            axis=0,
        )

    def around(power):
        power = power + (pltpu.roll(power, 1, 0) + pltpu.roll(power, BLK - 1, 0))
        return power + (pltpu.roll(power, 1, 1) + pltpu.roll(power, BLK - 1, 1))

    def kernel(*rest):
        many = len(tiles)
        tile_refs, follow_refs, second_refs = (rest[i * many : (i + 1) * many] for i in range(3))
        al_ref, ar_ref, bl_ref, br_ref = rest[3 * many : 3 * many + 4]
        out_ref, buffer, sems = rest[3 * many + 4 + have :]
        for base in range(0, count, batch):
            batched = range(base, min(base + batch, count))
            pairs = []
            for s in batched:
                i, at = homes[s]
                t_re = tile_refs[i][at, 0].astype(F32)
                t_im = tile_refs[i][at, 1].astype(F32)
                for o in (follow_refs[i][at], second_refs[i][at]):
                    o_re = o[0].astype(F32)
                    o_im = o[1].astype(F32)
                    re = (t_re * o_re + t_im * o_im).astype(BF)
                    im = (t_im * o_re - t_re * o_im).astype(BF)
                    pairs.append(jnp.concatenate([re, im], axis=0))
            rows = aside(mm(al_ref[...], jnp.concatenate(pairs, axis=1)).astype(BF))
            spectrum = mm(rows, ar_ref[...])
            weighted = []
            for p in range(len(pairs)):
                s_re = spectrum[p * BLK : (p + 1) * BLK, :BLK]
                s_im = spectrum[p * BLK : (p + 1) * BLK, BLK:]
                power = s_re * s_re + s_im * s_im
                level = jnp.sum(jnp.sum(power, axis=0, keepdims=True), axis=1, keepdims=True)
                inverse = 1.0 / (9.0 * (level * (1.0 / (BLK * BLK)) + 1e-06))
                weight = lax.rsqrt(lax.rsqrt(around(power) * inverse))
                weighted.append(
                    jnp.concatenate([(s_re * weight).astype(BF), (s_im * weight).astype(BF)], axis=0)
                )
            back = aside(mm(bl_ref[...], jnp.concatenate(weighted, axis=1)).astype(BF))
            filtered = mm(back, br_ref[...]).astype(BF)
            for p in range(len(pairs)):
                for part in range(2):
                    buffer[base + p // 2, p % 2, part] = filtered[
                        p * BLK : (p + 1) * BLK, part * BLK : (part + 1) * BLK
                    ]
            for s in batched:
                pltpu.make_async_copy(buffer.at[s], out_ref.at[start + s], sems.at[s]).start()
        for s in range(count):
            pltpu.make_async_copy(buffer.at[s], out_ref.at[start + s], sems.at[s]).wait()

    anywhere = pl.BlockSpec(memory_space=pl.ANY)
    operands = [*tiles, *follows, *seconds, *tables] + ([result] if have else [])
    return pl.pallas_call(
        kernel,
        out_shape=jax.ShapeDtypeStruct((capacity, 2, 2, BLK, BLK), BF),
        in_specs=whole(3 * len(tiles) + 4) + [anywhere] * have,
        out_specs=anywhere,
        scratch_shapes=[
            pltpu.VMEM((count, 2, 2, BLK, BLK), BF),
            pltpu.SemaphoreType.DMA((count,)),
        ],
        input_output_aliases={len(operands) - 1: 0} if have else {},
        compiler_params=params(16),
        cost_estimate=cost(4 * count * 2 * 4 * 4 * BLK**3, operands + [*seconds] * 8),
        name="goldstein",
    )(*operands)


def body(echo_spectra, range_reference, azimuth_reference, block_owner, block_slot, kernel_index):
    shards = lax.axis_size("shard")
    dates = lax.axis_size("date")
    me = lax.axis_index("shard")
    date = lax.axis_index("date")
    info = jnp.concatenate(
        [block_owner[0], block_slot[0], kernel_index[0], jnp.stack([me, date]).astype(jnp.int32)]
    )
    cores = 2 if shards % 2 == 0 else 1
    chips = shards // cores
    total = block_owner.shape[1]
    group = total // shards
    capacity = 2 * group
    most = max(2, capacity // shards)
    group_columns = azimuth_reference.shape[2] // BLK
    plan = (shards, capacity, most, group, group_columns)
    rows = azimuth_reference.shape[1] // dates
    share = lax.dynamic_slice_in_dim(azimuth_reference, date * rows, rows, axis=1)
    shares = [share] + [hop(share, "shard", c, cores) for c in range(1, cores)]
    sent = filter_columns(shares, info, plan)
    echo = echo_spectra[0].astype(F32)
    real = (echo[0] * range_reference[0] + echo[1] * range_reference[1]).astype(BF)
    imag = (echo[1] * range_reference[0] - echo[0] * range_reference[1]).astype(BF)
    real, imag, sent = lax.optimization_barrier((real, imag, sent))
    got = [sent[0]] + [hop(sent[k], "shard", k * cores) for k in range(1, chips)]
    got = jnp.concatenate(got, axis=0)
    filters = [got] + [hop(got, "date", e) for e in range(1, dates)]
    compressed, blocks, columns = range_compress(real, imag, info, plan)
    parts = [compressed] + [hop(compressed, "shard", c, cores) for c in range(1, cores)]
    splits = ((2, 2, 2, 2), (4, 4)) if capacity == 16 else ((capacity,),)
    outbox = spread_columns(parts, columns, info, [sum(sizes) for sizes in splits], plan)
    tiles, follows, seconds = [], [], []
    start = 0
    for chunk, sizes in enumerate(splits):
        pieces = [outbox[chunk][0]] + [
            hop(outbox[chunk][k], "shard", k * cores) for k in range(1, chips)
        ]
        mine = focus(pieces, filters, blocks, info, start, cores, sizes, plan, 0)
        start += sum(sizes)
        if chunk:
            mine, follows[:1] = lax.optimization_barrier((mine, follows[:1]))
        for tile in mine:
            if dates == 4:
                second = hop(tile, "date", 2)
                follow = hop(jnp.where(date % 2 == 0, second, tile), "date", 1)
            else:
                second = shift(tile, "date", -2)
                follow = shift(tile, "date", -1)
            tiles.append(tile)
            follows.append(follow)
            seconds.append(second)
    result = None
    start = 0
    groups = [4, 1, 1] if len(tiles) == 6 else [len(tiles)]
    for group in groups:
        take = slice(0, group)
        mine = tiles[take], follows[take], seconds[take]
        result = goldstein(*mine, start, capacity, result)
        start += sum(tile.shape[0] for tile in mine[0])
        del tiles[take], follows[take], seconds[take]
    return result[None]


def solution(mesh):
    in_specs = (
        P(("grp", "date"), None, "shard", None),
        P(),
        P(None, None, "shard"),
        P(("grp", "date"), None),
        P(("grp", "date"), None),
        P(("grp", "date"), None),
    )
    out_specs = P(("grp", "date"), "shard", None, None, None, None)
    return jax.shard_map(body, mesh=mesh, in_specs=in_specs, out_specs=out_specs, check_vma=False)
```

```python
import math

import jax
import jax.numpy as jnp
import numpy as np
from jax import lax
from jax.experimental import pallas as pl
from jax.experimental.pallas import tpu as pltpu
from jax.sharding import PartitionSpec as P

BLK = 128
NSUB = 8
BF = jnp.bfloat16
F32 = jnp.float32
MIB = 1024 * 1024


def dft(rows, cols, size, sign, scale):
    phase = np.outer(np.arange(rows), np.arange(cols)) % size
    angle = 2.0 * np.pi / size * phase
    cosine = np.cos(angle) * scale
    sine = sign * np.sin(angle) * scale
    return np.block([[cosine, -sine], [sine, cosine]])


def kernel_taps():
    cells = np.arange(-3, 5)
    dist = cells[None, :] - (np.arange(NSUB)[:, None] + 0.5) / NSUB
    window = np.where(np.abs(dist) < 4.0, 0.5 + 0.5 * np.cos(np.pi * dist / 4.0), 0.0)
    return cells, np.sinc(dist) * window


def const(table):
    return jnp.asarray(table.astype(np.float32)).astype(BF)


def mm(left, right):
    return jnp.dot(left, right, preferred_element_type=F32)


def whole(count):
    return [pl.BlockSpec(memory_space=pltpu.VMEM)] * count


def loaded(arrays):
    def spec(shape):
        return pl.BlockSpec(shape, lambda *_: (0,) * len(shape))

    return [spec(a.shape) for a in arrays]


def params(mib):
    return pltpu.CompilerParams(vmem_limit_bytes=mib * MIB)


def cost(macs, arrays):
    size = sum(math.prod(a.shape) * a.dtype.itemsize for a in arrays)
    return pl.CostEstimate(flops=int(2 * macs), bytes_accessed=size, transcendentals=0)


def is_pow2(count):
    return count & (count - 1) == 0


def target_of(index, step, count):
    if is_pow2(count):
        return index ^ step
    return (index + step) % count


def source_of(index, step, count):
    if is_pow2(count):
        return index ^ step
    return (index + count - step) % count


def step_from(index, source, count):
    if is_pow2(count):
        return index ^ source
    return (index + count - source) % count


def hop(value, axis, step, within=None):
    count = lax.axis_size(axis)
    if within is None and axis == "shard" and count % 2 == 0:
        pairs = [(i, target_of(i // 2, step // 2, count // 2) * 2 + i % 2) for i in range(count)]
    else:
        size = within or count
        pairs = [(i, i // size * size + target_of(i % size, step, size)) for i in range(count)]
    return lax.ppermute(value, axis, pairs)


def shift(value, axis, steps):
    count = lax.axis_size(axis)
    return lax.ppermute(value, axis, [(i, (i + steps) % count) for i in range(count)])


def range_compress(real, imag, info, plan):
    pulses, samples = real.shape
    shards, capacity, most, group, group_columns = plan
    total = shards * group
    outer = samples // BLK
    first = dft(outer, outer, outer, 1, 1.0 / math.sqrt(outer))
    second = dft(outer, BLK, outer, 1, 1.0 / math.sqrt(BLK))
    phase = np.outer(np.arange(BLK), np.arange(BLK)) % samples
    angle = 2.0 * np.pi / samples * phase
    first = np.pad(first, ((0, 0), (0, BLK - 2 * outer)))
    rows = [np.cos(angle), np.sin(angle), first, second[:, :BLK], second[:, BLK:]]
    tables = jnp.asarray(np.concatenate(rows).astype(np.float32))
    spread = BLK // outer
    smem = pl.BlockSpec(memory_space=pltpu.SMEM)

    def arrange(info_ref, block_ref, place_ref, count_ref):
        for o in range(shards):
            for w in range(capacity):
                block_ref[o, w] = 0
                place_ref[o, w] = 0
            for g in range(shards):
                count_ref[g, o] = 0
        for b in range(total):
            owner = info_ref[b]
            rank = count_ref[b // group, owner]
            count_ref[b // group, owner] = rank + 1
            slot = info_ref[total + b]
            block_ref[owner, slot] = (b + 1) * most + rank
            place_ref[owner, slot] = b // group * group_columns + b % group % group_columns

    def kernel(info_ref, real_ref, imag_ref, tables_ref, *rest):
        out_ref, block_ref, place_ref, x_re, x_im, y_re, y_im, count_ref = rest
        arrange(info_ref, block_ref, place_ref, count_ref)
        at = 2 * BLK
        first_table = tables_ref[at : at + 2 * outer, : 2 * outer].astype(BF)
        at += 2 * outer
        second_table = jnp.concatenate(
            [tables_ref[at : at + 2 * outer, :], tables_ref[at + 2 * outer : at + 4 * outer, :]],
            axis=1,
        ).astype(BF)
        for j in range(outer):
            lanes = slice(j * BLK, (j + 1) * BLK)
            x_re[pl.ds(j, pulses, stride=outer), :] = real_ref[:, lanes].astype(F32)
            x_im[pl.ds(j, pulses, stride=outer), :] = imag_ref[:, lanes].astype(F32)
        turn_c = tables_ref[:BLK, :]
        turn_s = tables_ref[BLK : 2 * BLK, :]
        for q in range(pulses // 2):
            pair = []
            for p in (2 * q, 2 * q + 1):
                rows = slice(p * outer, (p + 1) * outer)
                pair.append(jnp.concatenate([x_re[rows, :], x_im[rows, :]], axis=0))
            section = mm(first_table, jnp.concatenate(pair, axis=1).astype(BF))
            turned = []
            for p in range(2):
                lanes = slice(p * BLK, (p + 1) * BLK)
                re = jnp.concatenate([section[:outer, lanes]] * spread, axis=0)
                im = jnp.concatenate([section[outer:, lanes]] * spread, axis=0)
                turned.append(
                    jnp.concatenate(
                        [re * turn_c - im * turn_s, re * turn_s + im * turn_c], axis=1
                    )
                )
            turned = jnp.concatenate(turned, axis=0).astype(BF)
            done = lax.dot_general(
                second_table, turned, (((1,), (1,)), ((), ())), preferred_element_type=F32
            )
            for p in range(2):
                lanes = slice(p * BLK, (p + 1) * BLK)
                rows = slice((2 * q + p) * outer, (2 * q + p + 1) * outer)
                y_re[rows, :] = done[:outer, lanes]
                y_im[rows, :] = done[outer:, lanes]
        for j in range(outer):
            rows = pl.ds(j, pulses, stride=outer)
            out_ref[0, j] = y_re[rows, :].astype(BF)
            out_ref[1, j] = y_im[rows, :].astype(BF)

    return pl.pallas_call(
        kernel,
        out_shape=[
            jax.ShapeDtypeStruct((2, outer, pulses, BLK), BF),
            jax.ShapeDtypeStruct((shards, capacity), jnp.int32),
            jax.ShapeDtypeStruct((shards, capacity), jnp.int32),
        ],
        in_specs=[smem] + whole(3),
        out_specs=[pl.BlockSpec(memory_space=pltpu.VMEM), smem, smem],
        scratch_shapes=[pltpu.VMEM((pulses * outer, BLK), F32)] * 4
        + [
            pltpu.SMEM((shards, shards), jnp.int32),
        ],
        compiler_params=params(16),
        cost_estimate=cost(
            pulses * 4 * BLK * outer * (outer + BLK), [real] * 6 + [tables]
        ),
        name="range_compress",
    )(info, real, imag, tables)


def spread_columns(parts, table, info, sizes, plan):
    _, _, pulses, _ = parts[0].shape
    cores = len(parts)
    shards, capacity, most, group, group_columns = plan
    chips = shards // cores
    chunks = len(sizes)

    def kernel(table_ref, info_ref, *rest):
        part_refs = rest[:cores]
        outs = rest[cores:]
        chip = info_ref[3 * shards * group] // cores
        core = info_ref[3 * shards * group] % cores
        for chunk in range(chunks):
            for k in range(chips):
                owner = target_of(chip, k, chips) * cores + core
                out = outs[chunk * chips + k]
                for s in range(sizes[chunk]):
                    column = table_ref[owner, sum(sizes[:chunk]) + s]
                    for c in range(cores):
                        at = source_of(core, c, cores) * pulses
                        rows = pl.ds(pl.multiple_of(at, pulses), pulses)
                        out[s, 0, rows, :] = part_refs[c][0, column]
                        out[s, 1, rows, :] = part_refs[c][1, column]

    pieces = [jax.ShapeDtypeStruct((size, 2, cores * pulses, BLK), BF) for size in sizes]
    smem = pl.BlockSpec(memory_space=pltpu.SMEM)
    outs = pl.pallas_call(
        kernel,
        out_shape=[piece for piece in pieces for _ in range(chips)],
        in_specs=[smem, smem] + whole(cores),
        out_specs=whole(chunks * chips),
        compiler_params=params(16),
        cost_estimate=cost(0, [*parts] * 2),
        name="spread_columns",
    )(table, info, *parts)
    return [outs[chunk * chips : (chunk + 1) * chips] for chunk in range(chunks)]


def filter_columns(parts, info, plan):
    _, rows, columns = parts[0].shape
    cores = len(parts)
    shards, _, most, group, group_columns = plan
    chips = shards // cores

    def kernel(info_ref, *rest):
        part_refs = rest[:cores]
        outs = rest[cores : cores + chips]
        column_ref, count_ref = rest[cores + chips :]
        chip = info_ref[3 * shards * group] // cores
        core = info_ref[3 * shards * group] % cores
        for c in range(cores):
            for o in range(shards):
                count_ref[c, o] = 0
                for r in range(most):
                    column_ref[c, o * most + r] = 0
            for b in range(group):
                owner = info_ref[(chip * cores + c) * group + b]
                rank = count_ref[c, owner]
                count_ref[c, owner] = rank + 1
                column_ref[c, owner * most + rank] = b % group_columns
        for k in range(chips):
            owner = target_of(chip, k, chips) * cores + core
            for c in range(cores):
                at = source_of(core, c, cores)
                for e in range(most):
                    column = column_ref[at, owner * most + e]
                    lanes = pl.ds(pl.multiple_of(column * BLK, BLK), BLK)
                    for part in range(2):
                        outs[k][at * most + e, part] = part_refs[c][part, :, lanes]

    piece = jax.ShapeDtypeStruct((cores * most, 2, rows, BLK), BF)
    smem = pl.BlockSpec(memory_space=pltpu.SMEM)
    return pl.pallas_call(
        kernel,
        out_shape=[piece] * chips,
        in_specs=[smem] + whole(cores),
        out_specs=whole(chips),
        scratch_shapes=[
            pltpu.SMEM((cores, shards * most), jnp.int32),
            pltpu.SMEM((cores, shards), jnp.int32),
        ],
        compiler_params=params(16),
        cost_estimate=cost(0, [*parts] * 2),
        name="filter_columns",
    )(info, *parts)


def resample_tables(forward):
    pulses = forward.shape[0] // 2
    rows = pulses // BLK
    cells, taps = kernel_taps()

    def kernel(forward_ref, out_ref):
        low, high = slice(0, pulses), slice(pulses, 2 * pulses)
        halves = [
            jnp.concatenate([forward_ref[low, side], forward_ref[high, side]], axis=1)
            for side in (low, high)
        ]
        down = lax.broadcasted_iota(jnp.int32, (BLK, BLK), 0)
        ahead = lax.broadcasted_iota(jnp.int32, (BLK, BLK), 1) - down
        for kind in range(NSUB):
            band = jnp.zeros((BLK, BLK), F32)
            for cell, tap in zip(cells, taps[kind]):
                band = jnp.where(ahead == int(cell), float(tap), band)
            band = band.astype(BF)
            for row in range(rows):
                for part in range(2):
                    mine = halves[part][row * BLK : (row + 1) * BLK]
                    out_ref[kind * rows + row, part * BLK : (part + 1) * BLK, :] = mm(
                        band, mine
                    ).astype(BF)

    shape = (NSUB * rows, 2 * BLK, 2 * pulses)
    return pl.pallas_call(
        kernel,
        out_shape=jax.ShapeDtypeStruct(shape, BF),
        in_specs=whole(1),
        out_specs=pl.BlockSpec(memory_space=pltpu.VMEM),
        compiler_params=params(16),
        cost_estimate=cost(math.prod(shape) * BLK, [forward] * 16),
        name="resample_tables",
    )(forward)


def focus(pieces, filters, table, info, start, cores, sizes, plan, forward, back):
    each, _, share, _ = pieces[0].shape
    chips = len(pieces)
    dates = len(filters)
    pulses = share * chips
    rows = filters[0].shape[-2]
    shards, _, most, group, group_columns = plan

    def kernel(info_ref, table_ref, forward_ref, back_ref, *rest):
        piece_refs = rest[:chips]
        filter_refs = rest[chips : chips + dates]
        outs = rest[chips + dates : chips + dates + len(sizes)]
        col, fil = rest[chips + dates + len(sizes) :]
        homes = [(i, s) for i, size in enumerate(sizes) for s in range(size)]
        chip = info_ref[3 * shards * group] // cores
        entries, table_rows, valid = [], [], []
        for s in range(each):
            code = table_ref[info_ref[3 * shards * group], start + s]
            block = code // most - 1
            valid.append(block >= 0)
            block = jnp.maximum(block, 0)
            sender = block // group
            step = step_from(chip, sender // cores, chips)
            entries.append((step * cores + sender % cores) * most + code % most)
            row = info_ref[2 * shards * group + block] * (pulses // BLK)
            row = row + block % group // group_columns
            table_rows.append(row)
        for k in range(chips):
            source = source_of(chip, k, chips)
            at = pl.multiple_of(source * share, share)
            for s in range(each):
                for part in range(2):
                    col[s, part, pl.ds(at, share), :] = piece_refs[k][s, part]
        for e in range(dates):
            at = pl.multiple_of(source_of(info_ref[3 * shards * group + 1], e, dates) * rows, rows)
            for s in range(each):
                for part in range(2):
                    fil[s, part, pl.ds(at, rows), :] = filter_refs[e][entries[s], part]
        for s in range(0, each, 2):
            both = [col[t].reshape(2 * pulses, BLK) for t in (s, s + 1)]
            doppler = mm(forward_ref[...], jnp.concatenate(both, axis=1))
            for t in (0, 1):
                lanes = slice(t * BLK, (t + 1) * BLK)
                re = doppler[:pulses, lanes]
                im = doppler[pulses:, lanes]
                a = fil[s + t, 0].astype(F32)
                b = fil[s + t, 1].astype(F32)
                shaped = jnp.concatenate([re * a - im * b, re * b + im * a], axis=0).astype(BF)
                image = mm(back_ref[table_rows[s + t]], shaped)
                image = jnp.where(valid[s + t], image, 0.0).astype(BF)
                i, at = homes[s + t]
                outs[i][at, 0] = image[:BLK]
                outs[i][at, 1] = image[BLK:]

    smem = pl.BlockSpec(memory_space=pltpu.SMEM)
    return pl.pallas_call(
        kernel,
        out_shape=[jax.ShapeDtypeStruct((size, 2, BLK, BLK), BF) for size in sizes],
        in_specs=[smem] * 2 + whole(2 + chips + dates),
        out_specs=whole(len(sizes)),
        scratch_shapes=[
            pltpu.VMEM((each, 2, pulses, BLK), BF),
            pltpu.VMEM((each, 2, pulses, BLK), BF),
        ],
        compiler_params=params(16),
        cost_estimate=cost(
            4 * each * 4 * pulses * (pulses + BLK) * BLK, [*pieces, *filters, forward, back] * 4
        ),
        name="focus",
    )(info, table, forward, back, *pieces, *filters)


def goldstein(tiles, follows, seconds, start, capacity, result):
    sizes = [tile.shape[0] for tile in tiles]
    count = sum(sizes)
    homes = [(i, s) for i, size in enumerate(sizes) for s in range(size)]
    scale = 1.0 / math.sqrt(BLK)
    ahead = dft(BLK, BLK, BLK, -1, scale)
    behind = dft(BLK, BLK, BLK, 1, scale)
    tables = [const(ahead), const(ahead.T), const(behind), const(behind.T)]
    have = 0 if result is None else 1
    batch = 4

    def aside(left):
        pairs = left.shape[1] // BLK
        return jnp.concatenate(
            [
                jnp.concatenate(
                    [left[:BLK, p * BLK : (p + 1) * BLK], left[BLK:, p * BLK : (p + 1) * BLK]],
                    axis=1,
                )
                for p in range(pairs)
            ],
            axis=0,
        )

    def around(power):
        power = power + (pltpu.roll(power, 1, 0) + pltpu.roll(power, BLK - 1, 0))
        return power + (pltpu.roll(power, 1, 1) + pltpu.roll(power, BLK - 1, 1))

    def kernel(*rest):
        many = len(tiles)
        tile_refs, follow_refs, second_refs = (rest[i * many : (i + 1) * many] for i in range(3))
        al_ref, ar_ref, bl_ref, br_ref = rest[3 * many : 3 * many + 4]
        out_ref, buffer, sems = rest[3 * many + 4 + have :]
        for base in range(0, count, batch):
            batched = range(base, min(base + batch, count))
            pairs = []
            for s in batched:
                i, at = homes[s]
                t_re = tile_refs[i][at, 0].astype(F32)
                t_im = tile_refs[i][at, 1].astype(F32)
                for o in (follow_refs[i][at], second_refs[i][at]):
                    o_re = o[0].astype(F32)
                    o_im = o[1].astype(F32)
                    re = (t_re * o_re + t_im * o_im).astype(BF)
                    im = (t_im * o_re - t_re * o_im).astype(BF)
                    pairs.append(jnp.concatenate([re, im], axis=0))
            rows = aside(mm(al_ref[...], jnp.concatenate(pairs, axis=1)).astype(BF))
            spectrum = mm(rows, ar_ref[...])
            weighted = []
            for p in range(len(pairs)):
                s_re = spectrum[p * BLK : (p + 1) * BLK, :BLK]
                s_im = spectrum[p * BLK : (p + 1) * BLK, BLK:]
                power = s_re * s_re + s_im * s_im
                level = jnp.sum(jnp.sum(power, axis=0, keepdims=True), axis=1, keepdims=True)
                inverse = 1.0 / (9.0 * (level * (1.0 / (BLK * BLK)) + 1e-06))
                weight = lax.rsqrt(lax.rsqrt(around(power) * inverse))
                weighted.append(
                    jnp.concatenate([(s_re * weight).astype(BF), (s_im * weight).astype(BF)], axis=0)
                )
            back = aside(mm(bl_ref[...], jnp.concatenate(weighted, axis=1)).astype(BF))
            filtered = mm(back, br_ref[...]).astype(BF)
            for p in range(len(pairs)):
                for part in range(2):
                    buffer[base + p // 2, p % 2, part] = filtered[
                        p * BLK : (p + 1) * BLK, part * BLK : (part + 1) * BLK
                    ]
            for s in batched:
                pltpu.make_async_copy(buffer.at[s], out_ref.at[start + s], sems.at[s]).start()
        for s in range(count):
            pltpu.make_async_copy(buffer.at[s], out_ref.at[start + s], sems.at[s]).wait()

    anywhere = pl.BlockSpec(memory_space=pl.ANY)
    operands = [*tiles, *follows, *seconds, *tables] + ([result] if have else [])
    return pl.pallas_call(
        kernel,
        out_shape=jax.ShapeDtypeStruct((capacity, 2, 2, BLK, BLK), BF),
        in_specs=whole(3 * len(tiles) + 4) + [anywhere] * have,
        out_specs=anywhere,
        scratch_shapes=[
            pltpu.VMEM((count, 2, 2, BLK, BLK), BF),
            pltpu.SemaphoreType.DMA((count,)),
        ],
        input_output_aliases={len(operands) - 1: 0} if have else {},
        compiler_params=params(16),
        cost_estimate=cost(4 * count * 2 * 4 * 4 * BLK**3, operands + [*seconds] * 8),
        name="goldstein",
    )(*operands)


def body(echo_spectra, range_reference, azimuth_reference, block_owner, block_slot, kernel_index):
    shards = lax.axis_size("shard")
    dates = lax.axis_size("date")
    me = lax.axis_index("shard")
    date = lax.axis_index("date")
    info = jnp.concatenate(
        [block_owner[0], block_slot[0], kernel_index[0], jnp.stack([me, date]).astype(jnp.int32)]
    )
    cores = 2 if shards % 2 == 0 else 1
    chips = shards // cores
    total = block_owner.shape[1]
    group = total // shards
    capacity = 2 * group
    most = max(2, capacity // shards)
    group_columns = azimuth_reference.shape[2] // BLK
    plan = (shards, capacity, most, group, group_columns)
    rows = azimuth_reference.shape[1] // dates
    share = lax.dynamic_slice_in_dim(azimuth_reference, date * rows, rows, axis=1)
    shares = [share] + [hop(share, "shard", c, cores) for c in range(1, cores)]
    sent = filter_columns(shares, info, plan)
    echo = echo_spectra[0].astype(F32)
    real = (echo[0] * range_reference[0] + echo[1] * range_reference[1]).astype(BF)
    imag = (echo[1] * range_reference[0] - echo[0] * range_reference[1]).astype(BF)
    real, imag, sent = lax.optimization_barrier((real, imag, sent))
    got = [sent[0]] + [hop(sent[k], "shard", k * cores) for k in range(1, chips)]
    got = jnp.concatenate(got, axis=0)
    filters = [got] + [hop(got, "date", e) for e in range(1, dates)]
    compressed, blocks, columns = range_compress(real, imag, info, plan)
    parts = [compressed] + [hop(compressed, "shard", c, cores) for c in range(1, cores)]
    splits = ((2, 4, 2), (4, 4)) if capacity == 16 else ((capacity,),)
    outbox = spread_columns(parts, columns, info, [sum(sizes) for sizes in splits], plan)
    pulses = echo_spectra.shape[2] * shards
    forward = const(dft(pulses, pulses, pulses, -1, 1.0 / math.sqrt(pulses)))
    back = resample_tables(forward)
    tiles, follows, seconds = [], [], []
    result, done = None, 0
    start = 0
    for chunk, sizes in enumerate(splits):
        pieces = [outbox[chunk][0]] + [
            hop(outbox[chunk][k], "shard", k * cores) for k in range(1, chips)
        ]
        mine = focus(pieces, filters, blocks, info, start, cores, sizes, plan, forward, back)
        start += sum(sizes)
        if chunk:
            mine, seconds[:1] = lax.optimization_barrier((mine, seconds[:1]))
        for i, tile in enumerate(mine):
            held = chunk and i == len(sizes) - 1
            if dates == 4:
                second = hop(tile, "date", 2)
                sent_on = jnp.where(date % 2 == 0, second, tile)
                if held:
                    sent_on, result = lax.optimization_barrier((sent_on, result))
                follow = hop(sent_on, "date", 1)
            else:
                second = shift(tile, "date", -2)
                follow = shift(tile, "date", -1)
            tiles.append(tile)
            follows.append(follow)
            seconds.append(second)
        groups = [1] * len(sizes) if chunk else [len(sizes)]
        for group in groups:
            take = slice(done, done + group)
            pieces = tiles[take], follows[take], seconds[take]
            at = sum(tile.shape[0] for tile in tiles[:done])
            result = goldstein(*pieces, at, capacity, result)
            done += group
    return result[None]


def solution(mesh):
    in_specs = (
        P(("grp", "date"), None, "shard", None),
        P(),
        P(None, None, "shard"),
        P(("grp", "date"), None),
        P(("grp", "date"), None),
        P(("grp", "date"), None),
    )
    out_specs = P(("grp", "date"), "shard", None, None, None, None)
    return jax.shard_map(body, mesh=mesh, in_specs=in_specs, out_specs=out_specs, check_vma=False)
```

```python
import math

import jax
import jax.numpy as jnp
import numpy as np
from jax import lax
from jax.experimental import pallas as pl
from jax.experimental.pallas import tpu as pltpu
from jax.sharding import PartitionSpec as P

BLK = 128
NSUB = 8
BF = jnp.bfloat16
F32 = jnp.float32
MIB = 1024 * 1024


def dft(rows, cols, size, sign, scale):
    phase = np.outer(np.arange(rows), np.arange(cols)) % size
    angle = 2.0 * np.pi / size * phase
    cosine = np.cos(angle) * scale
    sine = sign * np.sin(angle) * scale
    return np.block([[cosine, -sine], [sine, cosine]])


def kernel_taps():
    cells = np.arange(-3, 5)
    dist = cells[None, :] - (np.arange(NSUB)[:, None] + 0.5) / NSUB
    window = np.where(np.abs(dist) < 4.0, 0.5 + 0.5 * np.cos(np.pi * dist / 4.0), 0.0)
    return cells, np.sinc(dist) * window


def const(table):
    return jnp.asarray(table.astype(np.float32)).astype(BF)


def mm(left, right):
    return jnp.dot(left, right, preferred_element_type=F32)


def whole(count):
    return [pl.BlockSpec(memory_space=pltpu.VMEM)] * count


def loaded(arrays):
    def spec(shape):
        return pl.BlockSpec(shape, lambda *_: (0,) * len(shape))

    return [spec(a.shape) for a in arrays]


def params(mib):
    return pltpu.CompilerParams(vmem_limit_bytes=mib * MIB)


def cost(macs, arrays):
    size = sum(math.prod(a.shape) * a.dtype.itemsize for a in arrays)
    return pl.CostEstimate(flops=int(2 * macs), bytes_accessed=size, transcendentals=0)


def is_pow2(count):
    return count & (count - 1) == 0


def target_of(index, step, count):
    if is_pow2(count):
        return index ^ step
    return (index + step) % count


def source_of(index, step, count):
    if is_pow2(count):
        return index ^ step
    return (index + count - step) % count


def step_from(index, source, count):
    if is_pow2(count):
        return index ^ source
    return (index + count - source) % count


def hop(value, axis, step, within=None):
    count = lax.axis_size(axis)
    if within is None and axis == "shard" and count % 2 == 0:
        pairs = [(i, target_of(i // 2, step // 2, count // 2) * 2 + i % 2) for i in range(count)]
    else:
        size = within or count
        pairs = [(i, i // size * size + target_of(i % size, step, size)) for i in range(count)]
    return lax.ppermute(value, axis, pairs)


def shift(value, axis, steps):
    count = lax.axis_size(axis)
    return lax.ppermute(value, axis, [(i, (i + steps) % count) for i in range(count)])


def range_compress(real, imag, info, plan):
    pulses, samples = real.shape
    shards, capacity, most, group, group_columns = plan
    total = shards * group
    outer = samples // BLK
    first = dft(outer, outer, outer, 1, 1.0 / math.sqrt(outer))
    second = dft(outer, BLK, outer, 1, 1.0 / math.sqrt(BLK))
    phase = np.outer(np.arange(BLK), np.arange(BLK)) % samples
    angle = 2.0 * np.pi / samples * phase
    first = np.pad(first, ((0, 0), (0, BLK - 2 * outer)))
    rows = [np.cos(angle), np.sin(angle), first, second[:, :BLK], second[:, BLK:]]
    tables = jnp.asarray(np.concatenate(rows).astype(np.float32))
    spread = BLK // outer
    smem = pl.BlockSpec(memory_space=pltpu.SMEM)

    def arrange(info_ref, block_ref, place_ref, count_ref):
        for o in range(shards):
            for w in range(capacity):
                block_ref[o, w] = 0
                place_ref[o, w] = 0
            for g in range(shards):
                count_ref[g, o] = 0
        for b in range(total):
            owner = info_ref[b]
            rank = count_ref[b // group, owner]
            count_ref[b // group, owner] = rank + 1
            slot = info_ref[total + b]
            block_ref[owner, slot] = (b + 1) * most + rank
            place_ref[owner, slot] = b // group * group_columns + b % group % group_columns

    def kernel(info_ref, real_ref, imag_ref, tables_ref, *rest):
        out_ref, block_ref, place_ref, x_re, x_im, y_re, y_im, count_ref = rest
        arrange(info_ref, block_ref, place_ref, count_ref)
        at = 2 * BLK
        first_table = tables_ref[at : at + 2 * outer, : 2 * outer].astype(BF)
        at += 2 * outer
        second_table = jnp.concatenate(
            [tables_ref[at : at + 2 * outer, :], tables_ref[at + 2 * outer : at + 4 * outer, :]],
            axis=1,
        ).astype(BF)
        for j in range(outer):
            lanes = slice(j * BLK, (j + 1) * BLK)
            x_re[pl.ds(j, pulses, stride=outer), :] = real_ref[:, lanes].astype(F32)
            x_im[pl.ds(j, pulses, stride=outer), :] = imag_ref[:, lanes].astype(F32)
        turn_c = tables_ref[:BLK, :]
        turn_s = tables_ref[BLK : 2 * BLK, :]
        for q in range(pulses // 2):
            pair = []
            for p in (2 * q, 2 * q + 1):
                rows = slice(p * outer, (p + 1) * outer)
                pair.append(jnp.concatenate([x_re[rows, :], x_im[rows, :]], axis=0))
            section = mm(first_table, jnp.concatenate(pair, axis=1).astype(BF))
            turned = []
            for p in range(2):
                lanes = slice(p * BLK, (p + 1) * BLK)
                re = jnp.concatenate([section[:outer, lanes]] * spread, axis=0)
                im = jnp.concatenate([section[outer:, lanes]] * spread, axis=0)
                turned.append(
                    jnp.concatenate(
                        [re * turn_c - im * turn_s, re * turn_s + im * turn_c], axis=1
                    )
                )
            turned = jnp.concatenate(turned, axis=0).astype(BF)
            done = lax.dot_general(
                second_table, turned, (((1,), (1,)), ((), ())), preferred_element_type=F32
            )
            for p in range(2):
                lanes = slice(p * BLK, (p + 1) * BLK)
                rows = slice((2 * q + p) * outer, (2 * q + p + 1) * outer)
                y_re[rows, :] = done[:outer, lanes]
                y_im[rows, :] = done[outer:, lanes]
        for j in range(outer):
            rows = pl.ds(j, pulses, stride=outer)
            out_ref[0, j] = y_re[rows, :].astype(BF)
            out_ref[1, j] = y_im[rows, :].astype(BF)

    return pl.pallas_call(
        kernel,
        out_shape=[
            jax.ShapeDtypeStruct((2, outer, pulses, BLK), BF),
            jax.ShapeDtypeStruct((shards, capacity), jnp.int32),
            jax.ShapeDtypeStruct((shards, capacity), jnp.int32),
        ],
        in_specs=[smem] + whole(3),
        out_specs=[pl.BlockSpec(memory_space=pltpu.VMEM), smem, smem],
        scratch_shapes=[pltpu.VMEM((pulses * outer, BLK), F32)] * 4
        + [
            pltpu.SMEM((shards, shards), jnp.int32),
        ],
        compiler_params=params(16),
        cost_estimate=cost(
            pulses * 4 * BLK * outer * (outer + BLK), [real] * 6 + [tables]
        ),
        name="range_compress",
    )(info, real, imag, tables)


def spread_columns(parts, table, info, sizes, plan):
    _, _, pulses, _ = parts[0].shape
    cores = len(parts)
    shards, capacity, most, group, group_columns = plan
    chips = shards // cores
    chunks = len(sizes)

    def kernel(table_ref, info_ref, *rest):
        part_refs = rest[:cores]
        outs = rest[cores:]
        chip = info_ref[3 * shards * group] // cores
        core = info_ref[3 * shards * group] % cores
        for chunk in range(chunks):
            for k in range(chips):
                owner = target_of(chip, k, chips) * cores + core
                out = outs[chunk * chips + k]
                for s in range(sizes[chunk]):
                    column = table_ref[owner, sum(sizes[:chunk]) + s]
                    for c in range(cores):
                        at = source_of(core, c, cores) * pulses
                        rows = pl.ds(pl.multiple_of(at, pulses), pulses)
                        out[s, 0, rows, :] = part_refs[c][0, column]
                        out[s, 1, rows, :] = part_refs[c][1, column]

    pieces = [jax.ShapeDtypeStruct((size, 2, cores * pulses, BLK), BF) for size in sizes]
    smem = pl.BlockSpec(memory_space=pltpu.SMEM)
    outs = pl.pallas_call(
        kernel,
        out_shape=[piece for piece in pieces for _ in range(chips)],
        in_specs=[smem, smem] + whole(cores),
        out_specs=whole(chunks * chips),
        compiler_params=params(16),
        cost_estimate=cost(0, [*parts] * 2),
        name="spread_columns",
    )(table, info, *parts)
    return [outs[chunk * chips : (chunk + 1) * chips] for chunk in range(chunks)]


def filter_columns(parts, info, plan):
    _, rows, columns = parts[0].shape
    cores = len(parts)
    shards, _, most, group, group_columns = plan
    chips = shards // cores

    def kernel(info_ref, *rest):
        part_refs = rest[:cores]
        outs = rest[cores : cores + chips]
        column_ref, count_ref = rest[cores + chips :]
        chip = info_ref[3 * shards * group] // cores
        core = info_ref[3 * shards * group] % cores
        for c in range(cores):
            for o in range(shards):
                count_ref[c, o] = 0
                for r in range(most):
                    column_ref[c, o * most + r] = 0
            for b in range(group):
                owner = info_ref[(chip * cores + c) * group + b]
                rank = count_ref[c, owner]
                count_ref[c, owner] = rank + 1
                column_ref[c, owner * most + rank] = b % group_columns
        for k in range(chips):
            owner = target_of(chip, k, chips) * cores + core
            for c in range(cores):
                at = source_of(core, c, cores)
                for e in range(most):
                    column = column_ref[at, owner * most + e]
                    lanes = pl.ds(pl.multiple_of(column * BLK, BLK), BLK)
                    for part in range(2):
                        outs[k][at * most + e, part] = part_refs[c][part, :, lanes]

    piece = jax.ShapeDtypeStruct((cores * most, 2, rows, BLK), BF)
    smem = pl.BlockSpec(memory_space=pltpu.SMEM)
    return pl.pallas_call(
        kernel,
        out_shape=[piece] * chips,
        in_specs=[smem] + whole(cores),
        out_specs=whole(chips),
        scratch_shapes=[
            pltpu.SMEM((cores, shards * most), jnp.int32),
            pltpu.SMEM((cores, shards), jnp.int32),
        ],
        compiler_params=params(16),
        cost_estimate=cost(0, [*parts] * 2),
        name="filter_columns",
    )(info, *parts)


def resample_tables(forward):
    pulses = forward.shape[0] // 2
    rows = pulses // BLK
    cells, taps = kernel_taps()

    def kernel(forward_ref, out_ref):
        low, high = slice(0, pulses), slice(pulses, 2 * pulses)
        halves = [
            jnp.concatenate([forward_ref[low, side], forward_ref[high, side]], axis=1)
            for side in (low, high)
        ]
        down = lax.broadcasted_iota(jnp.int32, (BLK, BLK), 0)
        ahead = lax.broadcasted_iota(jnp.int32, (BLK, BLK), 1) - down
        for kind in range(NSUB):
            band = jnp.zeros((BLK, BLK), F32)
            for cell, tap in zip(cells, taps[kind]):
                band = jnp.where(ahead == int(cell), float(tap), band)
            band = band.astype(BF)
            for row in range(rows):
                for part in range(2):
                    mine = halves[part][row * BLK : (row + 1) * BLK]
                    out_ref[kind * rows + row, part * BLK : (part + 1) * BLK, :] = mm(
                        band, mine
                    ).astype(BF)

    shape = (NSUB * rows, 2 * BLK, 2 * pulses)
    return pl.pallas_call(
        kernel,
        out_shape=jax.ShapeDtypeStruct(shape, BF),
        in_specs=whole(1),
        out_specs=pl.BlockSpec(memory_space=pltpu.VMEM),
        compiler_params=params(16),
        cost_estimate=cost(math.prod(shape) * BLK, [forward] * 16),
        name="resample_tables",
    )(forward)


def focus(pieces, filters, table, info, start, cores, sizes, plan, forward, back):
    each, _, share, _ = pieces[0].shape
    chips = len(pieces)
    dates = len(filters)
    pulses = share * chips
    rows = filters[0].shape[-2]
    shards, _, most, group, group_columns = plan

    def kernel(info_ref, table_ref, forward_ref, back_ref, *rest):
        piece_refs = rest[:chips]
        filter_refs = rest[chips : chips + dates]
        outs = rest[chips + dates : chips + dates + len(sizes)]
        col, fil = rest[chips + dates + len(sizes) :]
        homes = [(i, s) for i, size in enumerate(sizes) for s in range(size)]
        chip = info_ref[3 * shards * group] // cores
        entries, table_rows, valid = [], [], []
        for s in range(each):
            code = table_ref[info_ref[3 * shards * group], start + s]
            block = code // most - 1
            valid.append(block >= 0)
            block = jnp.maximum(block, 0)
            sender = block // group
            step = step_from(chip, sender // cores, chips)
            entries.append((step * cores + sender % cores) * most + code % most)
            row = info_ref[2 * shards * group + block] * (pulses // BLK)
            row = row + block % group // group_columns
            table_rows.append(row)
        for k in range(chips):
            source = source_of(chip, k, chips)
            at = pl.multiple_of(source * share, share)
            for s in range(each):
                for part in range(2):
                    col[s, part, pl.ds(at, share), :] = piece_refs[k][s, part]
        for e in range(dates):
            at = pl.multiple_of(source_of(info_ref[3 * shards * group + 1], e, dates) * rows, rows)
            for s in range(each):
                for part in range(2):
                    fil[s, part, pl.ds(at, rows), :] = filter_refs[e][entries[s], part]
        for s in range(0, each, 2):
            both = [col[t].reshape(2 * pulses, BLK) for t in (s, s + 1)]
            doppler = mm(forward_ref[...], jnp.concatenate(both, axis=1))
            for t in (0, 1):
                lanes = slice(t * BLK, (t + 1) * BLK)
                re = doppler[:pulses, lanes]
                im = doppler[pulses:, lanes]
                a = fil[s + t, 0].astype(F32)
                b = fil[s + t, 1].astype(F32)
                shaped = jnp.concatenate([re * a - im * b, re * b + im * a], axis=0).astype(BF)
                image = mm(back_ref[table_rows[s + t]], shaped)
                image = jnp.where(valid[s + t], image, 0.0).astype(BF)
                i, at = homes[s + t]
                outs[i][at, 0] = image[:BLK]
                outs[i][at, 1] = image[BLK:]

    smem = pl.BlockSpec(memory_space=pltpu.SMEM)
    return pl.pallas_call(
        kernel,
        out_shape=[jax.ShapeDtypeStruct((size, 2, BLK, BLK), BF) for size in sizes],
        in_specs=[smem] * 2 + whole(2 + chips + dates),
        out_specs=whole(len(sizes)),
        scratch_shapes=[
            pltpu.VMEM((each, 2, pulses, BLK), BF),
            pltpu.VMEM((each, 2, pulses, BLK), BF),
        ],
        compiler_params=params(16),
        cost_estimate=cost(
            11 * each * 4 * pulses * (pulses + BLK) * BLK, [*pieces, *filters, forward, back] * 8
        ),
        name="focus",
    )(info, table, forward, back, *pieces, *filters)


def goldstein(tiles, follows, seconds, start, capacity, result):
    sizes = [tile.shape[0] for tile in tiles]
    count = sum(sizes)
    homes = [(i, s) for i, size in enumerate(sizes) for s in range(size)]
    scale = 1.0 / math.sqrt(BLK)
    ahead = dft(BLK, BLK, BLK, -1, scale)
    behind = dft(BLK, BLK, BLK, 1, scale)
    tables = [const(ahead), const(ahead.T), const(behind), const(behind.T)]
    have = 0 if result is None else 1
    batch = 4

    def aside(left):
        pairs = left.shape[1] // BLK
        return jnp.concatenate(
            [
                jnp.concatenate(
                    [left[:BLK, p * BLK : (p + 1) * BLK], left[BLK:, p * BLK : (p + 1) * BLK]],
                    axis=1,
                )
                for p in range(pairs)
            ],
            axis=0,
        )

    def around(power):
        power = power + (pltpu.roll(power, 1, 0) + pltpu.roll(power, BLK - 1, 0))
        return power + (pltpu.roll(power, 1, 1) + pltpu.roll(power, BLK - 1, 1))

    def kernel(*rest):
        many = len(tiles)
        tile_refs, follow_refs, second_refs = (rest[i * many : (i + 1) * many] for i in range(3))
        al_ref, ar_ref, bl_ref, br_ref = rest[3 * many : 3 * many + 4]
        out_ref, buffer, sems = rest[3 * many + 4 + have :]
        for base in range(0, count, batch):
            batched = range(base, min(base + batch, count))
            pairs = []
            for s in batched:
                i, at = homes[s]
                t_re = tile_refs[i][at, 0].astype(F32)
                t_im = tile_refs[i][at, 1].astype(F32)
                for o in (follow_refs[i][at], second_refs[i][at]):
                    o_re = o[0].astype(F32)
                    o_im = o[1].astype(F32)
                    re = (t_re * o_re + t_im * o_im).astype(BF)
                    im = (t_im * o_re - t_re * o_im).astype(BF)
                    pairs.append(jnp.concatenate([re, im], axis=0))
            rows = aside(mm(al_ref[...], jnp.concatenate(pairs, axis=1)).astype(BF))
            spectrum = mm(rows, ar_ref[...])
            weighted = []
            for p in range(len(pairs)):
                s_re = spectrum[p * BLK : (p + 1) * BLK, :BLK]
                s_im = spectrum[p * BLK : (p + 1) * BLK, BLK:]
                power = s_re * s_re + s_im * s_im
                level = jnp.sum(jnp.sum(power, axis=0, keepdims=True), axis=1, keepdims=True)
                inverse = 1.0 / (9.0 * (level * (1.0 / (BLK * BLK)) + 1e-06))
                weight = lax.rsqrt(lax.rsqrt(around(power) * inverse))
                weighted.append(
                    jnp.concatenate([(s_re * weight).astype(BF), (s_im * weight).astype(BF)], axis=0)
                )
            back = aside(mm(bl_ref[...], jnp.concatenate(weighted, axis=1)).astype(BF))
            filtered = mm(back, br_ref[...]).astype(BF)
            for p in range(len(pairs)):
                for part in range(2):
                    buffer[base + p // 2, p % 2, part] = filtered[
                        p * BLK : (p + 1) * BLK, part * BLK : (part + 1) * BLK
                    ]
            for s in batched:
                pltpu.make_async_copy(buffer.at[s], out_ref.at[start + s], sems.at[s]).start()
        for s in range(count):
            pltpu.make_async_copy(buffer.at[s], out_ref.at[start + s], sems.at[s]).wait()

    anywhere = pl.BlockSpec(memory_space=pl.ANY)
    operands = [*tiles, *follows, *seconds, *tables] + ([result] if have else [])
    return pl.pallas_call(
        kernel,
        out_shape=jax.ShapeDtypeStruct((capacity, 2, 2, BLK, BLK), BF),
        in_specs=whole(3 * len(tiles) + 4) + [anywhere] * have,
        out_specs=anywhere,
        scratch_shapes=[
            pltpu.VMEM((count, 2, 2, BLK, BLK), BF),
            pltpu.SemaphoreType.DMA((count,)),
        ],
        input_output_aliases={len(operands) - 1: 0} if have else {},
        compiler_params=params(16),
        cost_estimate=cost(4 * count * 2 * 4 * 4 * BLK**3, operands + [*seconds] * 8),
        name="goldstein",
    )(*operands)


def body(echo_spectra, range_reference, azimuth_reference, block_owner, block_slot, kernel_index):
    shards = lax.axis_size("shard")
    dates = lax.axis_size("date")
    me = lax.axis_index("shard")
    date = lax.axis_index("date")
    info = jnp.concatenate(
        [block_owner[0], block_slot[0], kernel_index[0], jnp.stack([me, date]).astype(jnp.int32)]
    )
    cores = 2 if shards % 2 == 0 else 1
    chips = shards // cores
    total = block_owner.shape[1]
    group = total // shards
    capacity = 2 * group
    most = max(2, capacity // shards)
    group_columns = azimuth_reference.shape[2] // BLK
    plan = (shards, capacity, most, group, group_columns)
    rows = azimuth_reference.shape[1] // dates
    share = lax.dynamic_slice_in_dim(azimuth_reference, date * rows, rows, axis=1)
    shares = [share] + [hop(share, "shard", c, cores) for c in range(1, cores)]
    sent = filter_columns(shares, info, plan)
    echo = echo_spectra[0].astype(F32)
    real = (echo[0] * range_reference[0] + echo[1] * range_reference[1]).astype(BF)
    imag = (echo[1] * range_reference[0] - echo[0] * range_reference[1]).astype(BF)
    real, imag, sent = lax.optimization_barrier((real, imag, sent))
    got = [sent[0]] + [hop(sent[k], "shard", k * cores) for k in range(1, chips)]
    got = jnp.concatenate(got, axis=0)
    filters = [got] + [hop(got, "date", e) for e in range(1, dates)]
    compressed, blocks, columns = range_compress(real, imag, info, plan)
    parts = [compressed] + [hop(compressed, "shard", c, cores) for c in range(1, cores)]
    splits = ((2, 4, 2), (4, 4)) if capacity == 16 else ((capacity,),)
    outbox = spread_columns(parts, columns, info, [sum(sizes) for sizes in splits], plan)
    pulses = echo_spectra.shape[2] * shards
    forward = const(dft(pulses, pulses, pulses, -1, 1.0 / math.sqrt(pulses)))
    back = resample_tables(forward)
    tiles, follows, seconds = [], [], []
    result, done = None, 0
    start = 0
    for chunk, sizes in enumerate(splits):
        pieces = [outbox[chunk][0]] + [
            hop(outbox[chunk][k], "shard", k * cores) for k in range(1, chips)
        ]
        mine = focus(pieces, filters, blocks, info, start, cores, sizes, plan, forward, back)
        start += sum(sizes)
        if chunk:
            mine, seconds[:1] = lax.optimization_barrier((mine, seconds[:1]))
        for i, tile in enumerate(mine):
            held = chunk and i == len(sizes) - 1
            if dates == 4:
                second = hop(tile, "date", 2)
                sent_on = jnp.where(date % 2 == 0, second, tile)
                if held:
                    sent_on, result = lax.optimization_barrier((sent_on, result))
                follow = hop(sent_on, "date", 1)
            else:
                second = shift(tile, "date", -2)
                follow = shift(tile, "date", -1)
            tiles.append(tile)
            follows.append(follow)
            seconds.append(second)
        groups = [1] * len(sizes) if chunk else [len(sizes)]
        for group in groups:
            take = slice(done, done + group)
            pieces = tiles[take], follows[take], seconds[take]
            at = sum(tile.shape[0] for tile in tiles[:done])
            result = goldstein(*pieces, at, capacity, result)
            done += group
    return result[None]


def solution(mesh):
    in_specs = (
        P(("grp", "date"), None, "shard", None),
        P(),
        P(None, None, "shard"),
        P(("grp", "date"), None),
        P(("grp", "date"), None),
        P(("grp", "date"), None),
    )
    out_specs = P(("grp", "date"), "shard", None, None, None, None)
    return jax.shard_map(body, mesh=mesh, in_specs=in_specs, out_specs=out_specs, check_vma=False)
```

```python
import math

import jax
import jax.numpy as jnp
import numpy as np
from jax import lax
from jax.experimental import pallas as pl
from jax.experimental.pallas import tpu as pltpu
from jax.sharding import PartitionSpec as P

BLK = 128
NSUB = 8
BF = jnp.bfloat16
F32 = jnp.float32
MIB = 1024 * 1024


def dft(rows, cols, size, sign, scale):
    phase = np.outer(np.arange(rows), np.arange(cols)) % size
    angle = 2.0 * np.pi / size * phase
    cosine = np.cos(angle) * scale
    sine = sign * np.sin(angle) * scale
    return np.block([[cosine, -sine], [sine, cosine]])


def kernel_taps():
    cells = np.arange(-3, 5)
    dist = cells[None, :] - (np.arange(NSUB)[:, None] + 0.5) / NSUB
    window = np.where(np.abs(dist) < 4.0, 0.5 + 0.5 * np.cos(np.pi * dist / 4.0), 0.0)
    return cells, np.sinc(dist) * window


def const(table):
    return jnp.asarray(table.astype(np.float32)).astype(BF)


def mm(left, right):
    return jnp.dot(left, right, preferred_element_type=F32)


def whole(count):
    return [pl.BlockSpec(memory_space=pltpu.VMEM)] * count


def loaded(arrays):
    def spec(shape):
        return pl.BlockSpec(shape, lambda *_: (0,) * len(shape))

    return [spec(a.shape) for a in arrays]


def params(mib):
    return pltpu.CompilerParams(vmem_limit_bytes=mib * MIB)


def cost(macs, arrays):
    size = sum(math.prod(a.shape) * a.dtype.itemsize for a in arrays)
    return pl.CostEstimate(flops=int(2 * macs), bytes_accessed=size, transcendentals=0)


def is_pow2(count):
    return count & (count - 1) == 0


def target_of(index, step, count):
    if is_pow2(count):
        return index ^ step
    return (index + step) % count


def source_of(index, step, count):
    if is_pow2(count):
        return index ^ step
    return (index + count - step) % count


def step_from(index, source, count):
    if is_pow2(count):
        return index ^ source
    return (index + count - source) % count


def hop(value, axis, step, within=None):
    count = lax.axis_size(axis)
    if within is None and axis == "shard" and count % 2 == 0:
        pairs = [(i, target_of(i // 2, step // 2, count // 2) * 2 + i % 2) for i in range(count)]
    else:
        size = within or count
        pairs = [(i, i // size * size + target_of(i % size, step, size)) for i in range(count)]
    return lax.ppermute(value, axis, pairs)


def shift(value, axis, steps):
    count = lax.axis_size(axis)
    return lax.ppermute(value, axis, [(i, (i + steps) % count) for i in range(count)])


def range_compress(real, imag, info, plan):
    pulses, samples = real.shape
    shards, capacity, most, group, group_columns = plan
    total = shards * group
    outer = samples // BLK
    first = dft(outer, outer, outer, 1, 1.0 / math.sqrt(outer))
    second = dft(outer, BLK, outer, 1, 1.0 / math.sqrt(BLK))
    phase = np.outer(np.arange(BLK), np.arange(BLK)) % samples
    angle = 2.0 * np.pi / samples * phase
    first = np.pad(first, ((0, 0), (0, BLK - 2 * outer)))
    rows = [np.cos(angle), np.sin(angle), first, second[:, :BLK], second[:, BLK:]]
    tables = jnp.asarray(np.concatenate(rows).astype(np.float32))
    spread = BLK // outer
    smem = pl.BlockSpec(memory_space=pltpu.SMEM)

    def arrange(info_ref, block_ref, place_ref, count_ref):
        for o in range(shards):
            for w in range(capacity):
                block_ref[o, w] = 0
                place_ref[o, w] = 0
            for g in range(shards):
                count_ref[g, o] = 0
        for b in range(total):
            owner = info_ref[b]
            rank = count_ref[b // group, owner]
            count_ref[b // group, owner] = rank + 1
            slot = info_ref[total + b]
            block_ref[owner, slot] = (b + 1) * most + rank
            place_ref[owner, slot] = b // group * group_columns + b % group % group_columns

    def kernel(info_ref, real_ref, imag_ref, tables_ref, *rest):
        out_ref, block_ref, place_ref, x_re, x_im, y_re, y_im, count_ref = rest
        arrange(info_ref, block_ref, place_ref, count_ref)
        at = 2 * BLK
        first_table = tables_ref[at : at + 2 * outer, : 2 * outer].astype(BF)
        at += 2 * outer
        second_table = jnp.concatenate(
            [tables_ref[at : at + 2 * outer, :], tables_ref[at + 2 * outer : at + 4 * outer, :]],
            axis=1,
        ).astype(BF)
        for j in range(outer):
            lanes = slice(j * BLK, (j + 1) * BLK)
            x_re[pl.ds(j, pulses, stride=outer), :] = real_ref[:, lanes].astype(F32)
            x_im[pl.ds(j, pulses, stride=outer), :] = imag_ref[:, lanes].astype(F32)
        turn_c = tables_ref[:BLK, :]
        turn_s = tables_ref[BLK : 2 * BLK, :]
        for q in range(pulses // 2):
            pair = []
            for p in (2 * q, 2 * q + 1):
                rows = slice(p * outer, (p + 1) * outer)
                pair.append(jnp.concatenate([x_re[rows, :], x_im[rows, :]], axis=0))
            section = mm(first_table, jnp.concatenate(pair, axis=1).astype(BF))
            turned = []
            for p in range(2):
                lanes = slice(p * BLK, (p + 1) * BLK)
                re = jnp.concatenate([section[:outer, lanes]] * spread, axis=0)
                im = jnp.concatenate([section[outer:, lanes]] * spread, axis=0)
                turned.append(
                    jnp.concatenate(
                        [re * turn_c - im * turn_s, re * turn_s + im * turn_c], axis=1
                    )
                )
            turned = jnp.concatenate(turned, axis=0).astype(BF)
            done = lax.dot_general(
                second_table, turned, (((1,), (1,)), ((), ())), preferred_element_type=F32
            )
            for p in range(2):
                lanes = slice(p * BLK, (p + 1) * BLK)
                rows = slice((2 * q + p) * outer, (2 * q + p + 1) * outer)
                y_re[rows, :] = done[:outer, lanes]
                y_im[rows, :] = done[outer:, lanes]
        for j in range(outer):
            rows = pl.ds(j, pulses, stride=outer)
            out_ref[0, j] = y_re[rows, :].astype(BF)
            out_ref[1, j] = y_im[rows, :].astype(BF)

    return pl.pallas_call(
        kernel,
        out_shape=[
            jax.ShapeDtypeStruct((2, outer, pulses, BLK), BF),
            jax.ShapeDtypeStruct((shards, capacity), jnp.int32),
            jax.ShapeDtypeStruct((shards, capacity), jnp.int32),
        ],
        in_specs=[smem] + whole(3),
        out_specs=[pl.BlockSpec(memory_space=pltpu.VMEM), smem, smem],
        scratch_shapes=[pltpu.VMEM((pulses * outer, BLK), F32)] * 4
        + [
            pltpu.SMEM((shards, shards), jnp.int32),
        ],
        compiler_params=params(16),
        cost_estimate=cost(
            pulses * 4 * BLK * outer * (outer + BLK), [real] * 6 + [tables]
        ),
        name="range_compress",
    )(info, real, imag, tables)


def spread_columns(parts, table, info, sizes, plan):
    _, _, pulses, _ = parts[0].shape
    cores = len(parts)
    shards, capacity, most, group, group_columns = plan
    chips = shards // cores
    chunks = len(sizes)

    def kernel(table_ref, info_ref, *rest):
        part_refs = rest[:cores]
        outs = rest[cores:]
        chip = info_ref[3 * shards * group] // cores
        core = info_ref[3 * shards * group] % cores
        for chunk in range(chunks):
            for k in range(chips):
                owner = target_of(chip, k, chips) * cores + core
                out = outs[chunk * chips + k]
                for s in range(sizes[chunk]):
                    column = table_ref[owner, sum(sizes[:chunk]) + s]
                    for c in range(cores):
                        at = source_of(core, c, cores) * pulses
                        rows = pl.ds(pl.multiple_of(at, pulses), pulses)
                        out[s, 0, rows, :] = part_refs[c][0, column]
                        out[s, 1, rows, :] = part_refs[c][1, column]

    pieces = [jax.ShapeDtypeStruct((size, 2, cores * pulses, BLK), BF) for size in sizes]
    smem = pl.BlockSpec(memory_space=pltpu.SMEM)
    outs = pl.pallas_call(
        kernel,
        out_shape=[piece for piece in pieces for _ in range(chips)],
        in_specs=[smem, smem] + whole(cores),
        out_specs=whole(chunks * chips),
        compiler_params=params(16),
        cost_estimate=cost(0, [*parts] * 2),
        name="spread_columns",
    )(table, info, *parts)
    return [outs[chunk * chips : (chunk + 1) * chips] for chunk in range(chunks)]


def filter_columns(parts, info, plan):
    _, rows, columns = parts[0].shape
    cores = len(parts)
    shards, _, most, group, group_columns = plan
    chips = shards // cores

    def kernel(info_ref, *rest):
        part_refs = rest[:cores]
        outs = rest[cores : cores + chips]
        column_ref, count_ref = rest[cores + chips :]
        chip = info_ref[3 * shards * group] // cores
        core = info_ref[3 * shards * group] % cores
        for c in range(cores):
            for o in range(shards):
                count_ref[c, o] = 0
                for r in range(most):
                    column_ref[c, o * most + r] = 0
            for b in range(group):
                owner = info_ref[(chip * cores + c) * group + b]
                rank = count_ref[c, owner]
                count_ref[c, owner] = rank + 1
                column_ref[c, owner * most + rank] = b % group_columns
        for k in range(chips):
            owner = target_of(chip, k, chips) * cores + core
            for c in range(cores):
                at = source_of(core, c, cores)
                for e in range(most):
                    column = column_ref[at, owner * most + e]
                    lanes = pl.ds(pl.multiple_of(column * BLK, BLK), BLK)
                    for part in range(2):
                        outs[k][at * most + e, part] = part_refs[c][part, :, lanes]

    piece = jax.ShapeDtypeStruct((cores * most, 2, rows, BLK), BF)
    smem = pl.BlockSpec(memory_space=pltpu.SMEM)
    return pl.pallas_call(
        kernel,
        out_shape=[piece] * chips,
        in_specs=[smem] + whole(cores),
        out_specs=whole(chips),
        scratch_shapes=[
            pltpu.SMEM((cores, shards * most), jnp.int32),
            pltpu.SMEM((cores, shards), jnp.int32),
        ],
        compiler_params=params(16),
        cost_estimate=cost(0, [*parts] * 2),
        name="filter_columns",
    )(info, *parts)


def resample_tables(forward):
    pulses = forward.shape[0] // 2
    rows = pulses // BLK
    cells, taps = kernel_taps()

    def kernel(forward_ref, out_ref):
        low, high = slice(0, pulses), slice(pulses, 2 * pulses)
        halves = [
            jnp.concatenate([forward_ref[low, side], forward_ref[high, side]], axis=1)
            for side in (low, high)
        ]
        down = lax.broadcasted_iota(jnp.int32, (BLK, BLK), 0)
        ahead = lax.broadcasted_iota(jnp.int32, (BLK, BLK), 1) - down
        for kind in range(NSUB):
            band = jnp.zeros((BLK, BLK), F32)
            for cell, tap in zip(cells, taps[kind]):
                band = jnp.where(ahead == int(cell), float(tap), band)
            band = band.astype(BF)
            for row in range(rows):
                for part in range(2):
                    mine = halves[part][row * BLK : (row + 1) * BLK]
                    out_ref[kind * rows + row, part * BLK : (part + 1) * BLK, :] = mm(
                        band, mine
                    ).astype(BF)

    shape = (NSUB * rows, 2 * BLK, 2 * pulses)
    return pl.pallas_call(
        kernel,
        out_shape=jax.ShapeDtypeStruct(shape, BF),
        in_specs=whole(1),
        out_specs=pl.BlockSpec(memory_space=pltpu.VMEM),
        compiler_params=params(16),
        cost_estimate=cost(math.prod(shape) * BLK, [forward] * 16),
        name="resample_tables",
    )(forward)


def focus(pieces, filters, table, info, start, cores, sizes, plan, forward, back):
    each, _, share, _ = pieces[0].shape
    chips = len(pieces)
    dates = len(filters)
    pulses = share * chips
    rows = filters[0].shape[-2]
    shards, _, most, group, group_columns = plan

    def kernel(info_ref, table_ref, forward_ref, back_ref, *rest):
        piece_refs = rest[:chips]
        filter_refs = rest[chips : chips + dates]
        outs = rest[chips + dates : chips + dates + len(sizes)]
        col, fil = rest[chips + dates + len(sizes) :]
        homes = [(i, s) for i, size in enumerate(sizes) for s in range(size)]
        chip = info_ref[3 * shards * group] // cores
        entries, table_rows, valid = [], [], []
        for s in range(each):
            code = table_ref[info_ref[3 * shards * group], start + s]
            block = code // most - 1
            valid.append(block >= 0)
            block = jnp.maximum(block, 0)
            sender = block // group
            step = step_from(chip, sender // cores, chips)
            entries.append((step * cores + sender % cores) * most + code % most)
            row = info_ref[2 * shards * group + block] * (pulses // BLK)
            row = row + block % group // group_columns
            table_rows.append(row)
        for k in range(chips):
            source = source_of(chip, k, chips)
            at = pl.multiple_of(source * share, share)
            for s in range(each):
                for part in range(2):
                    col[s, part, pl.ds(at, share), :] = piece_refs[k][s, part]
        for e in range(dates):
            at = pl.multiple_of(source_of(info_ref[3 * shards * group + 1], e, dates) * rows, rows)
            for s in range(each):
                for part in range(2):
                    fil[s, part, pl.ds(at, rows), :] = filter_refs[e][entries[s], part]
        for s in range(0, each, 2):
            both = [col[t].reshape(2 * pulses, BLK) for t in (s, s + 1)]
            doppler = mm(forward_ref[...], jnp.concatenate(both, axis=1))
            for t in (0, 1):
                lanes = slice(t * BLK, (t + 1) * BLK)
                re = doppler[:pulses, lanes]
                im = doppler[pulses:, lanes]
                a = fil[s + t, 0].astype(F32)
                b = fil[s + t, 1].astype(F32)
                shaped = jnp.concatenate([re * a - im * b, re * b + im * a], axis=0).astype(BF)
                image = mm(back_ref[table_rows[s + t]], shaped)
                image = jnp.where(valid[s + t], image, 0.0).astype(BF)
                i, at = homes[s + t]
                outs[i][at, 0] = image[:BLK]
                outs[i][at, 1] = image[BLK:]

    smem = pl.BlockSpec(memory_space=pltpu.SMEM)
    return pl.pallas_call(
        kernel,
        out_shape=[jax.ShapeDtypeStruct((size, 2, BLK, BLK), BF) for size in sizes],
        in_specs=[smem] * 2 + whole(2 + chips + dates),
        out_specs=whole(len(sizes)),
        scratch_shapes=[
            pltpu.VMEM((each, 2, pulses, BLK), BF),
            pltpu.VMEM((each, 2, pulses, BLK), BF),
        ],
        compiler_params=params(16),
        cost_estimate=cost(
            11 * each * 4 * pulses * (pulses + BLK) * BLK, [*pieces, *filters, forward, back] * 8
        ),
        name="focus",
    )(info, table, forward, back, *pieces, *filters)


def goldstein(tiles, follows, seconds, start, capacity, result):
    sizes = [tile.shape[0] for tile in tiles]
    count = sum(sizes)
    homes = [(i, s) for i, size in enumerate(sizes) for s in range(size)]
    scale = 1.0 / math.sqrt(BLK)
    ahead = dft(BLK, BLK, BLK, -1, scale)
    behind = dft(BLK, BLK, BLK, 1, scale)
    tables = [const(ahead), const(ahead.T), const(behind), const(behind.T)]
    have = 0 if result is None else 1
    batch = 4

    def aside(left):
        pairs = left.shape[1] // BLK
        return jnp.concatenate(
            [
                jnp.concatenate(
                    [left[:BLK, p * BLK : (p + 1) * BLK], left[BLK:, p * BLK : (p + 1) * BLK]],
                    axis=1,
                )
                for p in range(pairs)
            ],
            axis=0,
        )

    def around(power):
        power = power + (pltpu.roll(power, 1, 0) + pltpu.roll(power, BLK - 1, 0))
        return power + (pltpu.roll(power, 1, 1) + pltpu.roll(power, BLK - 1, 1))

    def kernel(*rest):
        many = len(tiles)
        tile_refs, follow_refs, second_refs = (rest[i * many : (i + 1) * many] for i in range(3))
        al_ref, ar_ref, bl_ref, br_ref = rest[3 * many : 3 * many + 4]
        out_ref, buffer, sems = rest[3 * many + 4 + have :]
        for base in range(0, count, batch):
            batched = range(base, min(base + batch, count))
            pairs = []
            for s in batched:
                i, at = homes[s]
                t_re = tile_refs[i][at, 0].astype(F32)
                t_im = tile_refs[i][at, 1].astype(F32)
                for o in (follow_refs[i][at], second_refs[i][at]):
                    o_re = o[0].astype(F32)
                    o_im = o[1].astype(F32)
                    re = (t_re * o_re + t_im * o_im).astype(BF)
                    im = (t_im * o_re - t_re * o_im).astype(BF)
                    pairs.append(jnp.concatenate([re, im], axis=0))
            rows = aside(mm(al_ref[...], jnp.concatenate(pairs, axis=1)).astype(BF))
            spectrum = mm(rows, ar_ref[...])
            weighted = []
            for p in range(len(pairs)):
                s_re = spectrum[p * BLK : (p + 1) * BLK, :BLK]
                s_im = spectrum[p * BLK : (p + 1) * BLK, BLK:]
                power = s_re * s_re + s_im * s_im
                level = jnp.sum(jnp.sum(power, axis=0, keepdims=True), axis=1, keepdims=True)
                inverse = 1.0 / (9.0 * (level * (1.0 / (BLK * BLK)) + 1e-06))
                weight = lax.rsqrt(lax.rsqrt(around(power) * inverse))
                weighted.append(
                    jnp.concatenate([(s_re * weight).astype(BF), (s_im * weight).astype(BF)], axis=0)
                )
            back = aside(mm(bl_ref[...], jnp.concatenate(weighted, axis=1)).astype(BF))
            for n, s in enumerate(batched):
                mine = back[2 * n * BLK : 2 * (n + 1) * BLK]
                filtered = mm(mine, br_ref[...]).astype(BF)
                for p in range(2):
                    for part in range(2):
                        buffer[s, p, part] = filtered[
                            p * BLK : (p + 1) * BLK, part * BLK : (part + 1) * BLK
                        ]
                pltpu.make_async_copy(buffer.at[s], out_ref.at[start + s], sems.at[s]).start()
        for s in range(count):
            pltpu.make_async_copy(buffer.at[s], out_ref.at[start + s], sems.at[s]).wait()

    anywhere = pl.BlockSpec(memory_space=pl.ANY)
    operands = [*tiles, *follows, *seconds, *tables] + ([result] if have else [])
    return pl.pallas_call(
        kernel,
        out_shape=jax.ShapeDtypeStruct((capacity, 2, 2, BLK, BLK), BF),
        in_specs=whole(3 * len(tiles) + 4) + [anywhere] * have,
        out_specs=anywhere,
        scratch_shapes=[
            pltpu.VMEM((count, 2, 2, BLK, BLK), BF),
            pltpu.SemaphoreType.DMA((count,)),
        ],
        input_output_aliases={len(operands) - 1: 0} if have else {},
        compiler_params=params(16),
        cost_estimate=cost(4 * count * 2 * 4 * 4 * BLK**3, operands + [*seconds] * 8),
        name="goldstein",
    )(*operands)


def body(echo_spectra, range_reference, azimuth_reference, block_owner, block_slot, kernel_index):
    shards = lax.axis_size("shard")
    dates = lax.axis_size("date")
    me = lax.axis_index("shard")
    date = lax.axis_index("date")
    info = jnp.concatenate(
        [block_owner[0], block_slot[0], kernel_index[0], jnp.stack([me, date]).astype(jnp.int32)]
    )
    cores = 2 if shards % 2 == 0 else 1
    chips = shards // cores
    total = block_owner.shape[1]
    group = total // shards
    capacity = 2 * group
    most = max(2, capacity // shards)
    group_columns = azimuth_reference.shape[2] // BLK
    plan = (shards, capacity, most, group, group_columns)
    rows = azimuth_reference.shape[1] // dates
    share = lax.dynamic_slice_in_dim(azimuth_reference, date * rows, rows, axis=1)
    shares = [share] + [hop(share, "shard", c, cores) for c in range(1, cores)]
    sent = filter_columns(shares, info, plan)
    echo = echo_spectra[0].astype(F32)
    real = (echo[0] * range_reference[0] + echo[1] * range_reference[1]).astype(BF)
    imag = (echo[1] * range_reference[0] - echo[0] * range_reference[1]).astype(BF)
    real, imag, sent = lax.optimization_barrier((real, imag, sent))
    got = [sent[0]] + [hop(sent[k], "shard", k * cores) for k in range(1, chips)]
    got = jnp.concatenate(got, axis=0)
    filters = [got] + [hop(got, "date", e) for e in range(1, dates)]
    compressed, blocks, columns = range_compress(real, imag, info, plan)
    parts = [compressed] + [hop(compressed, "shard", c, cores) for c in range(1, cores)]
    splits = ((2, 4, 2), (4, 4)) if capacity == 16 else ((capacity,),)
    outbox = spread_columns(parts, columns, info, [sum(sizes) for sizes in splits], plan)
    pulses = echo_spectra.shape[2] * shards
    forward = const(dft(pulses, pulses, pulses, -1, 1.0 / math.sqrt(pulses)))
    back = resample_tables(forward)
    tiles, follows, seconds = [], [], []
    result, done = None, 0
    start = 0
    for chunk, sizes in enumerate(splits):
        pieces = [outbox[chunk][0]] + [
            hop(outbox[chunk][k], "shard", k * cores) for k in range(1, chips)
        ]
        mine = focus(pieces, filters, blocks, info, start, cores, sizes, plan, forward, back)
        start += sum(sizes)
        if chunk:
            mine, seconds[:1] = lax.optimization_barrier((mine, seconds[:1]))
        for i, tile in enumerate(mine):
            held = chunk and i == len(sizes) - 1
            if dates == 4:
                second = hop(tile, "date", 2)
                sent_on = jnp.where(date % 2 == 0, second, tile)
                if held:
                    sent_on, result = lax.optimization_barrier((sent_on, result))
                follow = hop(sent_on, "date", 1)
            else:
                second = shift(tile, "date", -2)
                follow = shift(tile, "date", -1)
            tiles.append(tile)
            follows.append(follow)
            seconds.append(second)
        groups = [1] * len(sizes) if chunk else [len(sizes)]
        for group in groups:
            take = slice(done, done + group)
            pieces = tiles[take], follows[take], seconds[take]
            at = sum(tile.shape[0] for tile in tiles[:done])
            result = goldstein(*pieces, at, capacity, result)
            done += group
    return result[None]


def solution(mesh):
    in_specs = (
        P(("grp", "date"), None, "shard", None),
        P(),
        P(None, None, "shard"),
        P(("grp", "date"), None),
        P(("grp", "date"), None),
        P(("grp", "date"), None),
    )
    out_specs = P(("grp", "date"), "shard", None, None, None, None)
    return jax.shard_map(body, mesh=mesh, in_specs=in_specs, out_specs=out_specs, check_vma=False)
```
